512 devices in a mesh: section: 16 (over y, x_hi, core), seq: 32 (over x_lo, z).
Axes of the slice: x: 4 (x_hi: 2, x_lo: 2; x = x_hi * 2 + x_lo), y: 4, z: 16, core: 2. Of those that a mesh axis runs over, the one named last changes fastest.
Arguments:
- saved_input: bfloat16 [16, 4096, 4096], P('section', 'seq'), may hold values from -6 to 6
- norm_gain: float32 [16, 4096], P('section'), may hold values from 0.25 to 1.75
- down_proj: bfloat16 [16, 4096, 512], P('section', 'seq'), may hold values from -0.09375 to 0.09375
- up_proj: bfloat16 [16, 512, 4096], P('section', None, 'seq'), may hold values from -0.25 to 0.25
- left_in: bfloat16 [16, 4096, 128], P('section', 'seq'), may hold values from -0.5 to 0.5
- right_in: bfloat16 [16, 4096, 128], P('section', 'seq'), may hold values from -6 to 6
- warm_right: bfloat16 [16, 4096, 128], P('section', 'seq'), may hold values from -6 to 6
- error_buffer: bfloat16 [16, 4096, 4096], P('section', 'seq'), may hold values from -4 to 4
- pair_lengths: int32 [16, 2], P('section'), may hold values from 512 to 2048, as said below
Outputs:
- new_error: bfloat16 [16, 4096, 4096], P('section', 'seq')
- left_out: bfloat16 [16, 4096, 128], P('section', 'seq')
- right_out: bfloat16 [16, 4096, 128], P('section', 'seq')
The draws below stay inside these ranges and needn't reach their ends.
Inputs may be any that keep to these rules, and one draw needn't show every extreme that they name: `pair_lengths`: in each section one of the two sequences has the full length 2048.
All inputs are finite; a program needn't handle non-finite values.
Results may differ from the reference program's by a relative error of at most 0.025.
Values may be sent and summed in bfloat16 or wider, within the bound.
A program may use at most 64 MiB of HBM per device.

```python
import jax
import jax.numpy as jnp
from jax import lax

D = 4096
R = 128
RL = 512
TOK_DEV = 128
TOKENS = 4096
SEQ = 2048
N_SECTION = 16
N_SEQ = 32


def draw_pair_lengths(key, part):
    key = jax.random.fold_in(key, 11)
    first_key, second_key = jax.random.split(key)
    base_lengths = jax.random.randint(first_key, (N_SECTION, 2), SEQ // 4, SEQ + 1)
    full_column = jax.random.randint(second_key, (N_SECTION, 1), 0, 2)
    columns = jnp.arange(2, dtype=jnp.int32)[None, :]
    return jnp.where(columns == full_column, SEQ, base_lengths).astype(jnp.int32)


def raised(drawn, key, source, target, shards_of, factor):
    owner, partner = [(jnp.arange(drawn.shape[dim]) // (drawn.shape[dim] // shards_of)).reshape([-1 if axis == dim else 1 for axis in range(drawn.ndim)]) for dim in (source, target)]
    chosen = jax.random.permutation(key, shards_of)[partner]
    strong = (owner == chosen) | (owner == (partner + shards_of // 2) % shards_of)
    return jnp.where(strong, factor * drawn, drawn)


def block_levels(own_key, shape, cuts, low, largest):
    loudness, own = 1.0, jax.random.fold_in(own_key, 6)
    for dim, shards_of in cuts:
        draws = jnp.exp(jax.random.uniform(jax.random.fold_in(own, dim), (shards_of,), jnp.float32, low / len(cuts), largest / len(cuts)))
        loudness = loudness * jnp.repeat(draws, shape[dim] // shards_of).reshape([-1 if axis == dim else 1 for axis in range(len(shape))])
    return loudness


def noise(own_key, extent, width, most, cuts=(), kind=jnp.bfloat16):
    result = jax.random.normal(own_key, extent, jnp.float32) * width
    if len(cuts) > 0:
        result = block_levels(own_key, extent, cuts, -0.22, 0.18) * result
    return jnp.clip(result, min=-most, max=most).astype(kind)


def bell_draw_with(rng, shape, scale, bound, shards, heavy, kind=jnp.bfloat16):
    values = scale * jax.random.normal(rng, shape, jnp.float32)
    if shards:
        values = values * block_levels(rng, shape, shards, -0.22, 0.18)
    return jnp.clip(raised(values, jax.random.fold_in(rng, 3), *heavy), -bound, bound).astype(kind)


def setup_inputs(seed: int = 0) -> dict:
    seeds = jax.random.split(jax.random.key(seed), 10)
    saved_input = noise(seeds[0], (N_SECTION, TOKENS, D), 1.0, 6.0, ((0, 16), (1, 32)))
    norm_gain = jnp.clip(1.0 + 0.15 * jax.random.normal(seeds[1], (N_SECTION, D), jnp.float32), 0.25, 1.75)
    down_proj = noise(seeds[2], (N_SECTION, D, RL), D ** -0.5, 0.09375, ((0, 16), (1, 32)))
    up_proj = noise(seeds[3], (N_SECTION, RL, D), RL ** -0.5, 0.25, ((0, 16), (2, 32)))
    left_in = noise(seeds[4], (N_SECTION, TOKENS, R), R ** -0.5, 0.5, ((0, 16), (1, 32)))
    right_in = noise(seeds[5], (N_SECTION, D, R), 1.0, 6.0, ((0, 16), (1, 32)))
    warm_right = noise(seeds[6], (N_SECTION, D, R), 1.0, 6.0, ((0, 16), (1, 32)))
    error_buffer = bell_draw_with(seeds[7], (N_SECTION, TOKENS, D), 0.5, 4.0, ((0, 16), (1, 32)), (1, 2, 32, 2.75))
    pair_lengths = draw_pair_lengths(jax.random.fold_in(seeds[9], 71), 0)
    return {"saved_input": saved_input, "norm_gain": norm_gain, "down_proj": down_proj, "up_proj": up_proj, "left_in": left_in, "right_in": right_in, "warm_right": warm_right, "error_buffer": error_buffer, "pair_lengths": pair_lengths}


def contract_last(left, right):
    return lax.dot_general(left.astype(jnp.float32), right.astype(jnp.float32), (((1,), (1,)), ((), ())), preferred_element_type=jnp.float32)

def section_pass(items):
    saved, gain, down, upper, left, right, warm, errors, lengths = items
    wide_input = saved.astype(jnp.float32)
    inv_rms = lax.rsqrt(lax.optimization_barrier(jnp.mean(wide_input * wide_input, axis=-1, keepdims=True)) + 1e-05)
    unit_rows = wide_input * inv_rms
    normed = (unit_rows * gain).astype(jnp.bfloat16)
    ghat = contract_last(left, right)
    branch_pre = jnp.dot(normed.astype(jnp.float32), down.astype(jnp.float32), preferred_element_type=jnp.float32)
    dact = contract_last(ghat.astype(jnp.bfloat16), upper)
    gate_sig = jax.nn.sigmoid(branch_pre)
    dpre = (dact * gate_sig * (1.0 + branch_pre * (1.0 - gate_sig))).astype(jnp.bfloat16)
    dnormed = contract_last(dpre, down)
    dunit = dnormed * gain
    dnorm = inv_rms * (dunit - unit_rows * lax.optimization_barrier(jnp.mean(dunit * unit_rows, axis=-1, keepdims=True)))
    position = jnp.arange(TOKENS, dtype=jnp.int32)
    which_seq = position // SEQ
    within = position % SEQ
    limit = jnp.where(which_seq == 0, lengths[0], lengths[1])
    live_rows = (within < limit).astype(jnp.float32)[:, None]
    moment = live_rows * (ghat + dnorm + errors.astype(jnp.float32))
    moment16 = moment.astype(jnp.bfloat16)
    projected = jnp.dot(moment16.astype(jnp.float32), warm.astype(jnp.float32), preferred_element_type=jnp.float32)
    gram_matrix = jnp.dot(projected.T, projected, precision=lax.Precision.HIGHEST)
    lower_factor = jnp.linalg.cholesky(gram_matrix)
    phat = lax.linalg.triangular_solve(lower_factor, projected, left_side=False, lower=True, transpose_a=True)
    phat16 = phat.astype(jnp.bfloat16)
    blocks_mom = moment16.reshape(N_SEQ, TOK_DEV, D).astype(jnp.float32)
    blocks_left = phat16.reshape(N_SEQ, TOK_DEV, R).astype(jnp.float32)
    partial_terms = jnp.einsum('nti,ntr->nir', blocks_mom, blocks_left, precision=lax.Precision.HIGHEST)
    rounded_terms = lax.optimization_barrier(partial_terms.astype(jnp.bfloat16))
    right16 = lax.optimization_barrier(jnp.sum(rounded_terms.astype(jnp.float32), axis=0)).astype(jnp.bfloat16)
    approx = contract_last(phat16, right16)
    new_error = (moment - approx).astype(jnp.bfloat16)
    return (new_error, phat16, right16)

def reference(saved_input, norm_gain, down_proj, up_proj, left_in, right_in, warm_right, error_buffer, pair_lengths):
    new_error, phat_all, right_all = lax.map(section_pass, (saved_input, norm_gain, down_proj, up_proj, left_in, right_in, warm_right, error_buffer, pair_lengths))
    left_out = jnp.concatenate([phat_all[1:], jnp.zeros_like(phat_all[:1])], axis=0)
    right_out = jnp.concatenate([right_all[1:], jnp.zeros_like(right_all[:1])], axis=0)
    return (new_error, left_out, right_out)
```

```python
import functools

import jax
import jax.numpy as jnp
from jax import lax
from jax.experimental import pallas as pl
from jax.experimental.pallas import tpu as pltpu
from jax.sharding import PartitionSpec as P

MESH = pl.DeviceIdType.MESH
HIGHEST = lax.Precision.HIGHEST
F32 = jnp.float32
BF16 = jnp.bfloat16
RIGHT, LEFT = 0, 1


def nt(a, b, precision=None):
    return lax.dot_general(
        a, b, (((1,), (1,)), ((), ())), preferred_element_type=F32, precision=precision
    )


def nn(a, b, precision=None):
    return jnp.dot(a, b, preferred_element_type=F32, precision=precision)


def split(a):
    hi = a.astype(BF16)
    return hi, (a - hi.astype(F32)).astype(BF16)


def kernel(
    n_section, nz, rank, lens, gain_in, saved, err, down, up, left, right, warm,
    out_ne, out_l, out_r,
    gain, xall, xoth, eall, lall, upv, dall, rw, ivb,
    mpart, ml1, m2s, ml2, mxs, mxr, mown, mfull,
    xg, prs, prr, pre_ref, dpre_ref, mom, mom16, pjs, pjr, pj,
    gpart, gl1, g2s, gl2, gfull, work, linv, ut, ula, ulb, u2s, un, ul2, rt, ph16, rown, neb,
    ld_sem, x_send, x_recv, a_send, a_recv,
    m_send, m_recv, g_send, g_recv, u_send, u_recv, r_send, r_recv, q_send, q_recv,
    ne_send, ne_recv, ne_loc, sec_send, sec_recv,
):
    tok = left.shape[0]
    feat = saved.shape[1]
    half = feat // 2
    steps = nz // 2
    chunk = 2 * tok
    n_chunk = half // chunk
    rl = down.shape[1]
    nb = 4
    na = nz // nb

    s = lax.axis_index("section")
    q = lax.axis_index("seq")
    x = q // nz
    z = lax.rem(q, nz)
    a = z // nb
    b = lax.rem(z, nb)
    o = 1 - x
    base = x * nz
    partner = o * nz + z
    zr = base + lax.rem(z + 1, nz)
    zl = base + lax.rem(z + nz - 1, nz)
    s_prev = lax.rem(s + n_section - 1, n_section)
    s_next = lax.rem(s + 1, n_section)

    def mod(i):
        return lax.rem(i + 2 * nz, nz)

    def rows(start, size):
        return pl.ds(pl.multiple_of(start, size), size)

    def near_b(k):
        return lax.rem(b + k, nb)

    def far_a(k):
        return lax.rem(a + k, na)

    mine = rows(x * tok, tok)
    theirs = rows(o * tok, tok)
    my_half = rows(x * half, half)
    other_half = rows(o * half, half)
    my_block = rows(z * tok, tok)

    loads = [
        pltpu.make_async_copy(src, dst, ld_sem.at[i])
        for i, (src, dst) in enumerate([
            (down, dall.at[my_block]),
            (right, rw.at[z, 0]),
            (warm, rw.at[z, 1]),
            (left, lall.at[mine]),
            (saved.at[:, other_half], xoth),
            (up, upv),
            (saved.at[:, my_half], xall.at[mine]),
            (err.at[:, my_half], eall.at[mine]),
            (gain_in, gain),
        ])
    ]
    for load in loads:
        load.start()

    barrier = pltpu.get_barrier_semaphore()
    peers = [{"seq": base + a * nb + near_b(k)} for k in range(1, nb)]
    peers += [{"seq": base + far_a(k) * nb + b} for k in range(1, na)]
    peers += [{"seq": zr}, {"seq": zl}, {"seq": partner}, {"section": s_prev}, {"section": s_next}]
    for peer in peers:
        pl.semaphore_signal(barrier, inc=1, device_id=peer, device_id_type=MESH)
    pl.semaphore_wait(barrier, len(peers))

    def send_to(device, src, dst, send, recv):
        return pltpu.make_async_remote_copy(
            src_ref=src, dst_ref=dst, send_sem=send, recv_sem=recv,
            device_id=device, device_id_type=MESH,
        )

    def across(i, src, dst):
        return send_to({"seq": partner}, src, dst, x_send.at[i], x_recv.at[i])

    def near(k, src, dst, send, recv):
        return send_to({"seq": base + a * nb + near_b(k)}, src, dst, send, recv)

    def far(k, src, dst, send, recv):
        return send_to({"seq": base + far_a(k) * nb + b}, src, dst, send, recv)

    def loop(first, end, fn):
        def body(k, _):
            fn(k)
            return 0

        lax.fori_loop(first, end, body, 0)

    longer = [(0, RIGHT), (1, LEFT)]

    def hop(stream, way, step):
        block = mod(z - step) if way == RIGHT else mod(z + step)
        ref = dall.at[rows(block * tok, tok)] if stream == 0 else rw.at[block]
        return send_to(
            {"seq": zr if way == RIGHT else zl}, ref, ref,
            a_send.at[stream, way, step], a_recv.at[stream, way, step],
        )

    def has(stream, way, step):
        return step < (steps if (stream, way) in longer else steps - 1)

    def advance(stream, step):
        for way in (RIGHT, LEFT):
            if has(stream, way, step):
                hop(stream, way, step).wait_recv()
                if has(stream, way, step + 1):
                    hop(stream, way, step + 1).start()

    def ring_start(stream):
        for way in (RIGHT, LEFT):
            hop(stream, way, 0).start()

    loads[0].wait()
    ring_start(0)
    loads[1].wait()
    loads[2].wait()
    loads[3].wait()
    x_left = across(1, lall.at[mine], lall.at[mine])
    x_left.start()
    loads[4].wait()
    x_saved = across(0, xoth, xall.at[mine])
    x_saved.start()
    loads[5].wait()

    mb, ms = rl // nb, rl // nz
    mpart[...] = nn(upv[...], rw[z, 0]).astype(BF16)
    my_m = rows(b * mb + a * ms, ms)
    my_mb = rows(b * mb, mb)
    m1 = [near(k, mpart.at[rows(near_b(k) * mb, mb)], ml1.at[k], m_send.at[0, k], m_recv.at[0, k])
          for k in range(1, nb)]
    m2 = [far(k, m2s.at[rows(far_a(k) * ms, ms)], ml2.at[k], m_send.at[1, k], m_recv.at[1, k])
          for k in range(1, na)]
    m3 = [far(k, mown, mfull.at[my_m], m_send.at[2, k], m_recv.at[2, k]) for k in range(1, na)]
    m4 = [near(k, mfull.at[my_mb], mfull.at[my_mb], m_send.at[3, k], m_recv.at[3, k])
          for k in range(1, nb)]

    def start(copies):
        for copy in copies:
            copy.start()

    def arrive(copies):
        for copy in copies:
            copy.wait_recv()

    start(m1)
    x_err = across(2, err.at[:, other_half], eall.at[mine])
    x_err.start()

    loads[6].wait()
    total = jnp.zeros((tok, 1), F32)
    for c in range(half // 512):
        cols = pl.ds(c * 512, 512)
        for v in (xoth[:, cols], xall[mine, cols]):
            v = v.astype(F32)
            total = total + jnp.sum(v * v, axis=1, keepdims=True)
    ivb[mine, :] = jnp.broadcast_to(lax.rsqrt(total * (1.0 / feat) + 1e-05), (tok, 128))
    x_inv = across(3, ivb.at[mine], ivb.at[mine])
    x_inv.start()

    gain_off = x * half

    def scale(c):
        cols = rows(c * chunk, chunk)
        g = gain[:, rows(gain_off + c * chunk, chunk)]
        xg[:, cols] = (xall[:, cols].astype(F32) * g).astype(BF16)

    def term(block):
        return nn(xg[:, rows(block * tok, tok)], dall[rows(block * tok, tok), :])

    def blocks_of(step):
        if step < 0:
            return [z]
        if step == steps - 1:
            return [mod(z - steps)]
        return [mod(z - 1 - step), mod(z + 1 + step)]

    lag = 3 * steps // 8
    for t in range(steps):
        if t == lag:
            ring_start(1)
        advance(0, t)
        if t >= lag:
            advance(1, t - lag)
        if t == steps // 8:
            arrive(m1)
            msum = mpart[my_mb, :].astype(F32)
            for k in range(1, nb):
                msum = msum + ml1[k].astype(F32)
            m2s[...] = msum.astype(BF16)
            start(m2)
        if t == 3 * steps // 8:
            arrive(m2)
            msum = m2s[rows(a * ms, ms), :].astype(F32)
            for k in range(1, na):
                msum = msum + ml2[k].astype(F32)
            mxs[...] = msum
            x_m = across(4, mxs, mxr)
            x_m.start()
        if t == steps // 2:
            x_saved.wait_recv()
            loads[8].wait()
            loop(0, n_chunk, scale)
            pre_ref[...] = term(z)
        if t == 5 * steps // 8:
            x_m.wait_recv()
            mown[...] = (mxs[...] + mxr[...]).astype(BF16)
            mfull[my_m, :] = mown[...]
            start(m3)
        if t == 6 * steps // 8:
            arrive(m3)
            start(m4)
        if t >= steps // 2:
            first = 2 * (t - steps // 2)
            found = [term(block) for step in (first, first + 1) for block in blocks_of(step)]
            pre_own = pre_ref[...] + sum(found[1:], found[0])
            pre_ref[...] = pre_own
    prs[...] = pre_own.astype(BF16)
    x_pre = across(5, prs, prr)
    x_pre.start()

    x_left.wait_recv()
    share = -(-(steps + 1) // lag)
    for i in range(lag):
        advance(1, steps - lag + i)
        for step in range(i * share - 1, min((i + 1) * share, steps + 1) - 1):
            for block in blocks_of(step):
                mom[:, rows(block * tok, tok)] = nt(lall[...], rw[block, 0])
    x_inv.wait_recv()
    arrive(m4)
    dact = nt(lall[...], mfull[...])
    inv = ivb[:, 0:1]
    slot = z * tok + lax.broadcasted_iota(jnp.int32, (2 * tok, 1), 0)
    second = lax.broadcasted_iota(jnp.int32, (2 * tok, 1), 0) >= tok
    limit = jnp.where(second, lens[0, 1] + tok, lens[0, 0])
    live = jnp.where(slot < limit, 1.0, 0.0).astype(F32)

    loads[7].wait()
    x_err.wait_recv()
    x_pre.wait_recv()
    pre = inv * (pre_ref[...] + prr[...].astype(F32))
    sg = 1.0 / (1.0 + jnp.exp(-pre))
    dpre = (dact * sg * (1.0 + pre * (1.0 - sg))).astype(BF16)
    dpre_ref[...] = dpre
    mean = jnp.sum(dpre.astype(F32) * pre, axis=1, keepdims=True) * (1.0 / feat)
    back = inv * inv * mean
    pjs[...] = jnp.zeros_like(pjs)

    def momentum(c):
        cols = rows(c * chunk, chunk)
        g = gain[:, rows(gain_off + c * chunk, chunk)]
        dn = nt(dpre_ref[...], dall[cols, :])
        m = mom[:, cols] + eall[:, cols].astype(F32)
        m = live * (m + inv * (dn * g) - xall[:, cols].astype(F32) * back)
        mom[:, cols] = m
        m16 = m.astype(BF16)
        mom16[:, cols] = m16
        pjs[...] += nn(m16, rw[pl.ds(2 * c, 2), 1].reshape(chunk, rank))

    loop(0, n_chunk, momentum)
    x_pj = across(6, pjs, pjr)
    x_pj.start()
    x_pj.wait_recv()
    proj = pjs[...] + pjr[...]
    pj[...] = proj
    proj_t = proj.T

    gb = rank // nb
    my_gb = rows(b * gb, gb)
    gpart[...] = nn(proj_t, proj, HIGHEST)
    g1 = [near(k, gpart.at[rows(near_b(k) * gb, gb)], gl1.at[k], g_send.at[0, k], g_recv.at[0, k])
          for k in range(1, nb)]
    g2 = [far(k, g2s, gl2.at[k], g_send.at[1, k], g_recv.at[1, k]) for k in range(1, na)]
    g3 = [near(k, gfull.at[my_gb], gfull.at[my_gb], g_send.at[2, k], g_recv.at[2, k])
          for k in range(1, nb)]
    start(g1)

    hi, lo = split(proj_t)

    def moment_terms(j):
        residue = near_b(j)

        def terms(i):
            m = mom16[:, rows((i * nb + residue) * tok, tok)]
            ut[residue, i] = nn(hi, m) + nn(lo, m)

        loop(0, na, terms)

    first_half, last_half = pl.ds(0, na // 2), pl.ds(na // 2, na // 2)
    to_right, to_left = {"seq": zr}, {"seq": zl}
    ua = [
        send_to(to_right, ut.at[near_b(2), first_half], ula.at[0], u_send.at[0], u_recv.at[0]),
        send_to(to_left, ut.at[near_b(2), last_half], ula.at[1], u_send.at[1], u_recv.at[1]),
    ]
    ub = [
        send_to(to_right, ut.at[near_b(1)], ulb.at[0], u_send.at[2], u_recv.at[2]),
        send_to(to_left, ut.at[near_b(3)], ulb.at[1], u_send.at[3], u_recv.at[3]),
    ]
    u2 = [far(k, un.at[far_a(k)], ul2.at[k], u_send.at[3 + k], u_recv.at[3 + k])
          for k in range(1, na)]

    moment_terms(2)
    start(ua)
    arrive(g1)
    gsum = gpart[my_gb, :]
    for k in range(1, nb):
        gsum = gsum + gl1[k]
    g2s[...] = gsum
    start(g2)
    moment_terms(1)
    moment_terms(3)
    arrive(g2)
    gsum = g2s[...]
    for k in range(1, na):
        gsum = gsum + gl2[k]
    gfull[my_gb, :] = gsum
    start(g3)
    arrive(ua)
    ut[near_b(1), first_half] += ula[0]
    ut[near_b(3), last_half] += ula[1]
    start(ub)
    moment_terms(0)
    arrive(g3)
    work[...] = gfull[...]

    lane = lax.broadcasted_iota(jnp.int32, (1, rank), 1)
    group, width = 16, 8

    def eliminate(first, width):
        n = rank - first
        a = work[pl.ds(first, n), :]
        index = lax.broadcasted_iota(jnp.int32, (n, rank), 0)
        cols = [
            jnp.broadcast_to(a[:, first + k : first + k + 1], (n, rank)) for k in range(width)
        ]
        panel = a[0:8, :]
        rest = jnp.where((lane >= first) & (lane < first + width), 0.0, a)
        for k in range(width):
            here = lane == first + k
            pivot = cols[k][k : k + 1, :]
            factor = jnp.where(index > k, cols[k] * (1.0 / pivot), 0.0)
            unit = jnp.where(here, 1.0, panel[k : k + 1, :])
            linv[first + k : first + k + 1, :] = (
                jnp.where(lane <= first + k, unit, 0.0) * lax.rsqrt(pivot)
            )
            if k + 1 < width:
                panel = jnp.where(here, 0.0, panel) - factor[0:8, :] * unit
            for later in range(k + 1, width):
                cols[later] = cols[later] - factor * cols[k][later : later + 1, :]
            inside = (lane > first + k) & (lane < first + width)
            rest = rest - factor * jnp.where(inside, 0.0, unit)
        if n > width:
            work[pl.ds(first + width, n - width), :] = rest[width:, :]

    for first in range(0, rank // 2, width):
        eliminate(first, width)

    arrive(ub)
    u2s[...] = ut[b] + ulb[0] + ulb[1]
    for first in range(rank // 2, rank, width):
        eliminate(first, width)

    li = linv[...]
    for k in (*range(na // 2, na), *range(1, na // 2), 0):
        un[far_a(k)] = nn(li, u2s[far_a(k)], HIGHEST).astype(BF16)
        if k > 0:
            u2[k - 1].start()
    ph16[...] = nt(pj[...], li, HIGHEST).astype(BF16)
    to_prev = {"section": s_prev}
    outs = [
        send_to(to_prev, ph16.at[mine], out_l, sec_send.at[0], sec_recv.at[0]),
        send_to(to_prev, rown, out_r, sec_send.at[1], sec_recv.at[1]),
    ]
    outs[0].start()
    arrive(u2)
    right_t = un[a].astype(F32)
    for k in range(1, na):
        right_t = right_t + ul2[k].astype(F32)
    rt[b, a] = right_t.astype(BF16)

    r1 = [far(k, rt.at[b, a], rt.at[b, a], r_send.at[k], r_recv.at[k]) for k in range(1, na)]

    def pass_on(device, view, i):
        return send_to(device, rt.at[view], rt.at[view], q_send.at[i], q_recv.at[i])

    rb_right = [pass_on(to_right, (b, first_half), 0), pass_on(to_right, (b, last_half), 1)]
    rb_left = [pass_on(to_left, (b, first_half), 2), pass_on(to_left, (b, last_half), 3)]
    rc_right = pass_on(to_right, (near_b(3), first_half), 4)
    rc_left = pass_on(to_left, (near_b(1), last_half), 5)
    start(r1)
    rown[...] = right_t.T.astype(BF16)
    outs[1].start()
    arrive(r1)
    start([rb_right[0], rb_left[1], rb_right[1], rb_left[0]])

    def finished(block):
        cols = rows(block * tok, tok)
        return send_to(
            {"seq": partner}, neb.at[theirs, cols], out_ne.at[:, rows(x * half + block * tok, tok)],
            ne_send.at[block], ne_recv.at[block],
        )

    def finish(j, first, end):
        residue = near_b(j)

        def one(i):
            block = i * nb + residue
            cols = rows(block * tok, tok)
            approx = nn(ph16[...], rt[residue, i])
            neb[:, cols] = (mom[:, cols] - approx).astype(BF16)
            finished(block).start()

        loop(first, end, one)

    finish(0, 0, na)
    rb_right[0].wait_recv()
    rc_right.start()
    rb_left[1].wait_recv()
    rc_left.start()
    rb_right[1].wait_recv()
    finish(3, 0, na)
    rb_left[0].wait_recv()
    finish(1, 0, na)
    rc_right.wait_recv()
    finish(2, 0, na // 2)
    rc_left.wait_recv()
    finish(2, na // 2, na)
    own = pltpu.make_async_copy(neb.at[mine], out_ne.at[:, my_half], ne_loc)
    own.start()

    for copy in (x_saved, x_left, x_err, x_inv, x_m, x_pre, x_pj):
        copy.wait_send()
    for copies in (
        m1, m2, m3, m4, g1, g2, g3, ua, ub, u2, r1, rb_right, rb_left, [rc_right, rc_left],
    ):
        for copy in copies:
            copy.wait_send()

    def drain(step):
        for stream in (0, 1):
            for way in (RIGHT, LEFT):
                hop(stream, way, step).wait_send()

    loop(0, steps - 1, drain)
    for pair in longer:
        hop(*pair, steps - 1).wait_send()
    for copy in outs:
        copy.wait()
    loop(0, nz, lambda block: finished(block).wait_send())
    loop(0, nz, lambda block: finished(block).wait_recv())
    own.wait()


def per_device(
    n_section, nz, saved_input, norm_gain, down_proj, up_proj, left_in, right_in, warm_right,
    error_buffer, pair_lengths,
):
    tok, feat = saved_input.shape[1:]
    rank = left_in.shape[2]
    rl = down_proj.shape[2]
    half = feat // 2
    steps = nz // 2
    nb = 4
    na = nz // nb
    hbm = pl.BlockSpec(memory_space=pl.ANY)
    dma = pltpu.SemaphoreType.DMA
    vmem = pltpu.VMEM
    scratch = [
        vmem((1, feat), F32),
        vmem((2 * tok, half), BF16),
        vmem((tok, half), BF16),
        vmem((2 * tok, half), BF16),
        vmem((2 * tok, rank), BF16),
        vmem((rl, tok), BF16),
        vmem((half, rl), BF16),
        vmem((nz, 2, tok, rank), BF16),
        vmem((2 * tok, 128), F32),
        vmem((rl, rank), BF16),
        vmem((nb, rl // nb, rank), BF16),
        vmem((rl // nb, rank), BF16),
        vmem((na, rl // nz, rank), BF16),
        vmem((rl // nz, rank), F32),
        vmem((rl // nz, rank), F32),
        vmem((rl // nz, rank), BF16),
        vmem((rl, rank), BF16),
        vmem((2 * tok, half), BF16),
        vmem((2 * tok, rl), BF16),
        vmem((2 * tok, rl), BF16),
        vmem((2 * tok, rl), F32),
        vmem((2 * tok, rl), BF16),
        vmem((2 * tok, half), F32),
        vmem((2 * tok, half), BF16),
        vmem((2 * tok, rank), F32),
        vmem((2 * tok, rank), F32),
        vmem((2 * tok, rank), F32),
        vmem((rank, rank), F32),
        vmem((nb, rank // nb, rank), F32),
        vmem((rank // nb, rank), F32),
        vmem((na, rank // nb, rank), F32),
        vmem((rank, rank), F32),
        vmem((rank, rank), F32),
        vmem((rank, rank), F32),
        vmem((nb, na, rank, tok), F32),
        vmem((2, na // 2, rank, tok), F32),
        vmem((2, na, rank, tok), F32),
        vmem((na, rank, tok), F32),
        vmem((na, rank, tok), BF16),
        vmem((na, rank, tok), BF16),
        vmem((nb, na, rank, tok), BF16),
        vmem((2 * tok, rank), BF16),
        vmem((tok, rank), BF16),
        vmem((2 * tok, half), BF16),
        dma((9,)), dma((7,)), dma((7,)),
        dma((2, 2, steps)), dma((2, 2, steps)),
        dma((4, 4)), dma((4, 4)), dma((4, 4)), dma((4, 4)),
        dma((8,)), dma((8,)), dma((4,)), dma((4,)), dma((6,)), dma((6,)),
        dma((nz,)), dma((nz,)), dma, dma((2,)), dma((2,)),
    ]
    new_error, left_back, right_back = pl.pallas_call(
        functools.partial(kernel, n_section, nz, rank),
        out_shape=(
            jax.ShapeDtypeStruct((tok, feat), BF16),
            jax.ShapeDtypeStruct((tok, rank), BF16),
            jax.ShapeDtypeStruct((tok, rank), BF16),
        ),
        in_specs=[
            pl.BlockSpec(memory_space=pltpu.SMEM), hbm,
            hbm, hbm, hbm, hbm, hbm, hbm, hbm,
        ],
        out_specs=(hbm, hbm, hbm),
        scratch_shapes=scratch,
        compiler_params=pltpu.CompilerParams(
            collective_id=0, has_side_effects=True, vmem_limit_bytes=60 * 1024 * 1024
        ),
    )(
        pair_lengths, norm_gain, saved_input[0], error_buffer[0], down_proj[0], up_proj[0],
        left_in[0], right_in[0], warm_right[0],
    )
    keep = lax.axis_index("section") < n_section - 1
    left_back = jnp.where(keep, left_back, jnp.zeros_like(left_back))
    right_back = jnp.where(keep, right_back, jnp.zeros_like(right_back))
    return (new_error[None], left_back[None], right_back[None])


def solution(mesh):
    n_section = mesh.shape["section"]
    nz = mesh.shape["seq"] // 2
    return jax.shard_map(
        functools.partial(per_device, n_section, nz),
        mesh=mesh,
        in_specs=(
            P("section", "seq", None),
            P("section", None),
            P("section", "seq", None),
            P("section", None, "seq"),
            P("section", "seq", None),
            P("section", "seq", None),
            P("section", "seq", None),
            P("section", "seq", None),
            P("section", None),
        ),
        out_specs=(P("section", "seq", None), P("section", "seq", None), P("section", "seq", None)),
        check_vma=False,
    )
```

```python
import functools

import jax
import jax.numpy as jnp
from jax import lax
from jax.experimental import pallas as pl
from jax.experimental.pallas import tpu as pltpu
from jax.sharding import PartitionSpec as P

MESH = pl.DeviceIdType.MESH
HIGHEST = lax.Precision.HIGHEST
F32 = jnp.float32
BF16 = jnp.bfloat16
RIGHT, LEFT = 0, 1


def nt(a, b, precision=None):
    return lax.dot_general(
        a, b, (((1,), (1,)), ((), ())), preferred_element_type=F32, precision=precision
    )


def nn(a, b, precision=None):
    return jnp.dot(a, b, preferred_element_type=F32, precision=precision)


def split(a):
    hi = a.astype(BF16)
    return hi, (a - hi.astype(F32)).astype(BF16)


def kernel(
    n_section, nz, rank, lens, gain_in, saved, err, down, up, left, right, warm,
    out_ne, out_l, out_r,
    gain, xall, xoth, eall, lall, upv, dall, rw, ivb,
    mpart, ml1, m2s, ml2, mxs, mxr, mown, mfull,
    xg, prs, prr, pre_ref, dpre_ref, mom, mom16, pjs, pjr, pj,
    gpart, gl1, g2s, gl2, gfull, work, linv, ut, ula, ulb, u2s, un, ul2, rt, ph16, rown, neb,
    ld_sem, x_send, x_recv, a_send, a_recv,
    m_send, m_recv, g_send, g_recv, u_send, u_recv, r_send, r_recv, q_send, q_recv,
    ne_send, ne_recv, ne_loc, sec_send, sec_recv,
):
    tok = left.shape[0]
    feat = saved.shape[1]
    half = feat // 2
    steps = nz // 2
    chunk = 2 * tok
    n_chunk = half // chunk
    rl = down.shape[1]
    nb = 4
    na = nz // nb

    s = lax.axis_index("section")
    q = lax.axis_index("seq")
    x = q // nz
    z = lax.rem(q, nz)
    a = z // nb
    b = lax.rem(z, nb)
    o = 1 - x
    base = x * nz
    partner = o * nz + z
    zr = base + lax.rem(z + 1, nz)
    zl = base + lax.rem(z + nz - 1, nz)
    s_prev = lax.rem(s + n_section - 1, n_section)
    s_next = lax.rem(s + 1, n_section)

    def mod(i):
        return lax.rem(i + 2 * nz, nz)

    def rows(start, size):
        return pl.ds(pl.multiple_of(start, size), size)

    def near_b(k):
        return lax.rem(b + k, nb)

    def far_a(k):
        return lax.rem(a + k, na)

    mine = rows(x * tok, tok)
    theirs = rows(o * tok, tok)
    my_half = rows(x * half, half)
    other_half = rows(o * half, half)
    my_block = rows(z * tok, tok)

    loads = [
        pltpu.make_async_copy(src, dst, ld_sem.at[i])
        for i, (src, dst) in enumerate([
            (down, dall.at[my_block]),
            (right, rw.at[z, 0]),
            (warm, rw.at[z, 1]),
            (left, lall.at[mine]),
            (saved.at[:, other_half], xoth),
            (up, upv),
            (saved.at[:, my_half], xall.at[mine]),
            (err.at[:, my_half], eall.at[mine]),
            (gain_in, gain),
        ])
    ]
    for load in loads:
        load.start()

    barrier = pltpu.get_barrier_semaphore()
    peers = [{"seq": base + a * nb + near_b(k)} for k in range(1, nb)]
    peers += [{"seq": base + far_a(k) * nb + b} for k in range(1, na)]
    peers += [{"seq": zr}, {"seq": zl}, {"seq": partner}, {"section": s_prev}, {"section": s_next}]
    for peer in peers:
        pl.semaphore_signal(barrier, inc=1, device_id=peer, device_id_type=MESH)
    pl.semaphore_wait(barrier, len(peers))

    def send_to(device, src, dst, send, recv):
        return pltpu.make_async_remote_copy(
            src_ref=src, dst_ref=dst, send_sem=send, recv_sem=recv,
            device_id=device, device_id_type=MESH,
        )

    def across(i, src, dst):
        return send_to({"seq": partner}, src, dst, x_send.at[i], x_recv.at[i])

    def near(k, src, dst, send, recv):
        return send_to({"seq": base + a * nb + near_b(k)}, src, dst, send, recv)

    def far(k, src, dst, send, recv):
        return send_to({"seq": base + far_a(k) * nb + b}, src, dst, send, recv)

    def loop(first, end, fn):
        def body(k, _):
            fn(k)
            return 0

        lax.fori_loop(first, end, body, 0)

    longer = [(0, RIGHT), (1, LEFT)]

    def hop(stream, way, step):
        block = mod(z - step) if way == RIGHT else mod(z + step)
        ref = dall.at[rows(block * tok, tok)] if stream == 0 else rw.at[block]
        return send_to(
            {"seq": zr if way == RIGHT else zl}, ref, ref,
            a_send.at[stream, way, step], a_recv.at[stream, way, step],
        )

    def has(stream, way, step):
        return step < (steps if (stream, way) in longer else steps - 1)

    def advance(stream, step):
        for way in (RIGHT, LEFT):
            if has(stream, way, step):
                hop(stream, way, step).wait_recv()
                if has(stream, way, step + 1):
                    hop(stream, way, step + 1).start()

    def ring_start(stream):
        for way in (RIGHT, LEFT):
            hop(stream, way, 0).start()

    loads[0].wait()
    ring_start(0)
    loads[1].wait()
    loads[2].wait()
    loads[3].wait()
    x_left = across(1, lall.at[mine], lall.at[mine])
    x_left.start()
    loads[4].wait()
    x_saved = across(0, xoth, xall.at[mine])
    x_saved.start()
    loads[5].wait()

    mb, ms = rl // nb, rl // nz
    mpart[...] = nn(upv[...], rw[z, 0]).astype(BF16)
    my_m = rows(b * mb + a * ms, ms)
    my_mb = rows(b * mb, mb)
    m1 = [near(k, mpart.at[rows(near_b(k) * mb, mb)], ml1.at[k], m_send.at[0, k], m_recv.at[0, k])
          for k in range(1, nb)]
    m2 = [far(k, m2s.at[rows(far_a(k) * ms, ms)], ml2.at[k], m_send.at[1, k], m_recv.at[1, k])
          for k in range(1, na)]
    m3 = [far(k, mown, mfull.at[my_m], m_send.at[2, k], m_recv.at[2, k]) for k in range(1, na)]
    m4 = [near(k, mfull.at[my_mb], mfull.at[my_mb], m_send.at[3, k], m_recv.at[3, k])
          for k in range(1, nb)]

    def start(copies):
        for copy in copies:
            copy.start()

    def arrive(copies):
        for copy in copies:
            copy.wait_recv()

    start(m1)
    x_err = across(2, err.at[:, other_half], eall.at[mine])
    x_err.start()

    loads[6].wait()

    def squares(c, total):
        cols = rows(c * 128, 128)
        for v in (xoth[:, cols], xall[mine, cols]):
            v = v.astype(F32)
            total = total + v * v
        return total

    total = lax.fori_loop(0, half // 128, squares, jnp.zeros((tok, 128), F32))
    total = jnp.sum(total, axis=1, keepdims=True)
    ivb[mine, :] = jnp.broadcast_to(lax.rsqrt(total * (1.0 / feat) + 1e-05), (tok, 128))
    x_inv = across(3, ivb.at[mine], ivb.at[mine])
    x_inv.start()

    gain_off = x * half

    def scale(c):
        cols = rows(c * chunk, chunk)
        g = gain[:, rows(gain_off + c * chunk, chunk)]
        xg[:, cols] = (xall[:, cols].astype(F32) * g).astype(BF16)

    def term(block):
        return nn(xg[:, rows(block * tok, tok)], dall[rows(block * tok, tok), :])

    def add_terms(step):
        pre_ref[...] += term(mod(z - 1 - step)) + term(mod(z + 1 + step))

    def gradient(block):
        mom[:, rows(block * tok, tok)] = nt(lall[...], rw[block, 0])

    def gradients(step):
        gradient(mod(z - 1 - step))
        gradient(mod(z + 1 + step))

    lag = 3 * steps // 8
    for t in range(steps):
        if t == lag:
            ring_start(1)
        advance(0, t)
        if t >= lag:
            advance(1, t - lag)
        if t == steps // 8:
            arrive(m1)
            msum = mpart[my_mb, :].astype(F32)
            for k in range(1, nb):
                msum = msum + ml1[k].astype(F32)
            m2s[...] = msum.astype(BF16)
            start(m2)
        if t == 3 * steps // 8:
            arrive(m2)
            msum = m2s[rows(a * ms, ms), :].astype(F32)
            for k in range(1, na):
                msum = msum + ml2[k].astype(F32)
            mxs[...] = msum
            x_m = across(4, mxs, mxr)
            x_m.start()
        if t == steps // 2:
            x_saved.wait_recv()
            loads[8].wait()
            loop(0, n_chunk, scale)
            pre_ref[...] = term(z)
        if t == 5 * steps // 8:
            x_m.wait_recv()
            mown[...] = (mxs[...] + mxr[...]).astype(BF16)
            mfull[my_m, :] = mown[...]
            start(m3)
        if t == 6 * steps // 8:
            arrive(m3)
            start(m4)
        if t >= steps // 2:
            first = 2 * (t - steps // 2)
            loop(first, min(first + 2, steps - 1), add_terms)
    pre_own = pre_ref[...] + term(mod(z - steps))
    pre_ref[...] = pre_own
    prs[...] = pre_own.astype(BF16)
    x_pre = across(5, prs, prr)
    x_pre.start()

    x_left.wait_recv()
    gradient(z)
    for i in range(lag):
        advance(1, steps - lag + i)
        loop(i * steps // lag, min((i + 1) * steps // lag, steps - 1), gradients)
    gradient(mod(z - steps))
    x_inv.wait_recv()
    arrive(m4)
    dact = nt(lall[...], mfull[...])
    inv = ivb[:, 0:1]
    slot = z * tok + lax.broadcasted_iota(jnp.int32, (2 * tok, 1), 0)
    second = lax.broadcasted_iota(jnp.int32, (2 * tok, 1), 0) >= tok
    limit = jnp.where(second, lens[0, 1] + tok, lens[0, 0])
    live = jnp.where(slot < limit, 1.0, 0.0).astype(F32)

    loads[7].wait()
    x_err.wait_recv()
    x_pre.wait_recv()
    pre = inv * (pre_ref[...] + prr[...].astype(F32))
    sg = 1.0 / (1.0 + jnp.exp(-pre))
    dpre = (dact * sg * (1.0 + pre * (1.0 - sg))).astype(BF16)
    dpre_ref[...] = dpre
    mean = jnp.sum(dpre.astype(F32) * pre, axis=1, keepdims=True) * (1.0 / feat)
    back = inv * inv * mean
    pjs[...] = jnp.zeros_like(pjs)

    def momentum(c):
        cols = rows(c * chunk, chunk)
        g = gain[:, rows(gain_off + c * chunk, chunk)]
        dn = nt(dpre_ref[...], dall[cols, :])
        m = mom[:, cols] + eall[:, cols].astype(F32)
        m = live * (m + inv * (dn * g) - xall[:, cols].astype(F32) * back)
        mom[:, cols] = m
        m16 = m.astype(BF16)
        mom16[:, cols] = m16
        pjs[...] += nn(m16, rw[pl.ds(2 * c, 2), 1].reshape(chunk, rank))

    loop(0, n_chunk, momentum)
    x_pj = across(6, pjs, pjr)
    x_pj.start()
    x_pj.wait_recv()
    proj = pjs[...] + pjr[...]
    pj[...] = proj
    proj_t = proj.T

    gb = rank // nb
    my_gb = rows(b * gb, gb)
    gpart[...] = nn(proj_t, proj, HIGHEST)
    g1 = [near(k, gpart.at[rows(near_b(k) * gb, gb)], gl1.at[k], g_send.at[0, k], g_recv.at[0, k])
          for k in range(1, nb)]
    g2 = [far(k, g2s, gl2.at[k], g_send.at[1, k], g_recv.at[1, k]) for k in range(1, na)]
    g3 = [near(k, gfull.at[my_gb], gfull.at[my_gb], g_send.at[2, k], g_recv.at[2, k])
          for k in range(1, nb)]
    start(g1)

    hi, lo = split(proj_t)

    def moment_terms(j):
        residue = near_b(j)

        def terms(i):
            m = mom16[:, rows((i * nb + residue) * tok, tok)]
            ut[residue, i] = nn(hi, m) + nn(lo, m)

        loop(0, na, terms)

    first_half, last_half = pl.ds(0, na // 2), pl.ds(na // 2, na // 2)
    to_right, to_left = {"seq": zr}, {"seq": zl}
    ua = [
        send_to(to_right, ut.at[near_b(2), first_half], ula.at[0], u_send.at[0], u_recv.at[0]),
        send_to(to_left, ut.at[near_b(2), last_half], ula.at[1], u_send.at[1], u_recv.at[1]),
    ]
    ub = [
        send_to(to_right, ut.at[near_b(1)], ulb.at[0], u_send.at[2], u_recv.at[2]),
        send_to(to_left, ut.at[near_b(3)], ulb.at[1], u_send.at[3], u_recv.at[3]),
    ]
    u2 = [far(k, un.at[far_a(k)], ul2.at[k], u_send.at[3 + k], u_recv.at[3 + k])
          for k in range(1, na)]

    moment_terms(2)
    start(ua)
    arrive(g1)
    gsum = gpart[my_gb, :]
    for k in range(1, nb):
        gsum = gsum + gl1[k]
    g2s[...] = gsum
    start(g2)
    moment_terms(1)
    moment_terms(3)
    arrive(g2)
    gsum = g2s[...]
    for k in range(1, na):
        gsum = gsum + gl2[k]
    gfull[my_gb, :] = gsum
    start(g3)
    arrive(ua)
    ut[near_b(1), first_half] += ula[0]
    ut[near_b(3), last_half] += ula[1]
    start(ub)
    moment_terms(0)
    arrive(g3)
    work[...] = gfull[...]

    lane = lax.broadcasted_iota(jnp.int32, (1, rank), 1)
    width = 8

    def eliminate(top, first):
        n = rank - top
        first = pl.multiple_of(first, width)
        rest = work[top:, :]
        panel = work[pl.ds(first, width), :]
        index = top + lax.broadcasted_iota(jnp.int32, (n, rank), 0)
        inner = lax.broadcasted_iota(jnp.int32, (width, rank), 0)
        turned = pltpu.roll(rest, rank - first, 1)
        turned_panel = pltpu.roll(panel, rank - first, 1)
        cols = [jnp.broadcast_to(turned[:, k : k + 1], (n, rank)) for k in range(width)]
        heads = [
            jnp.broadcast_to(turned_panel[:, k : k + 1], (width, rank)) for k in range(width)
        ]
        done = index < first + width
        rest = jnp.where((lane >= first) & (lane < first + width), 0.0, rest)
        for k in range(width):
            here = lane == first + k
            pivot = heads[k][k : k + 1, :]
            inverse = 1.0 / pivot
            factor = jnp.where(done, 0.0, cols[k] * inverse)
            head = jnp.where(inner > k, heads[k] * inverse, 0.0)
            unit = jnp.where(here, 1.0, panel[k : k + 1, :])
            linv[pl.ds(first + k, 1), :] = (
                jnp.where(lane <= first + k, unit, 0.0) * lax.rsqrt(pivot)
            )
            if k + 1 < width:
                panel = jnp.where(here, 0.0, panel) - head * unit
            for later in range(k + 1, width):
                other = heads[k][later : later + 1, :]
                cols[later] = cols[later] - factor * other
                heads[later] = heads[later] - head * other
            inside = (lane > first + k) & (lane < first + width)
            rest = rest - factor * jnp.where(inside, 0.0, unit)
        work[top:, :] = rest

    def eliminate_from(top, end):
        loop(top // width, end // width, lambda i: eliminate(top, i * width))

    eliminate_from(0, rank // 2)

    arrive(ub)
    u2s[...] = ut[b] + ulb[0] + ulb[1]
    eliminate_from(rank // 2, rank)

    li = linv[...]
    for k in (*range(na // 2, na), *range(1, na // 2), 0):
        un[far_a(k)] = nn(li, u2s[far_a(k)], HIGHEST).astype(BF16)
        if k > 0:
            u2[k - 1].start()
    ph16[...] = nt(pj[...], li, HIGHEST).astype(BF16)
    to_prev = {"section": s_prev}
    outs = [
        send_to(to_prev, ph16.at[mine], out_l, sec_send.at[0], sec_recv.at[0]),
        send_to(to_prev, rown, out_r, sec_send.at[1], sec_recv.at[1]),
    ]
    outs[0].start()
    arrive(u2)
    right_t = un[a].astype(F32)
    for k in range(1, na):
        right_t = right_t + ul2[k].astype(F32)
    rt[b, a] = right_t.astype(BF16)

    r1 = [far(k, rt.at[b, a], rt.at[b, a], r_send.at[k], r_recv.at[k]) for k in range(1, na)]

    def pass_on(device, view, i):
        return send_to(device, rt.at[view], rt.at[view], q_send.at[i], q_recv.at[i])

    rb_right = [pass_on(to_right, (b, first_half), 0), pass_on(to_right, (b, last_half), 1)]
    rb_left = [pass_on(to_left, (b, first_half), 2), pass_on(to_left, (b, last_half), 3)]
    rc_right = pass_on(to_right, (near_b(3), first_half), 4)
    rc_left = pass_on(to_left, (near_b(1), last_half), 5)
    start(r1)
    rown[...] = right_t.T.astype(BF16)
    outs[1].start()
    arrive(r1)
    start([rb_right[0], rb_left[1], rb_right[1], rb_left[0]])

    def finished(block):
        cols = rows(block * tok, tok)
        return send_to(
            {"seq": partner}, neb.at[theirs, cols], out_ne.at[:, rows(x * half + block * tok, tok)],
            ne_send.at[block], ne_recv.at[block],
        )

    def finish(j, first, end):
        residue = near_b(j)

        def one(i):
            block = i * nb + residue
            cols = rows(block * tok, tok)
            approx = nn(ph16[...], rt[residue, i])
            neb[:, cols] = (mom[:, cols] - approx).astype(BF16)
            finished(block).start()

        loop(first, end, one)

    finish(0, 0, na)
    rb_right[0].wait_recv()
    rc_right.start()
    rb_left[1].wait_recv()
    rc_left.start()
    rb_right[1].wait_recv()
    finish(3, 0, na)
    rb_left[0].wait_recv()
    finish(1, 0, na)
    rc_right.wait_recv()
    finish(2, 0, na // 2)
    rc_left.wait_recv()
    finish(2, na // 2, na)
    own = pltpu.make_async_copy(neb.at[mine], out_ne.at[:, my_half], ne_loc)
    own.start()

    for copy in (x_saved, x_left, x_err, x_inv, x_m, x_pre, x_pj):
        copy.wait_send()
    for copies in (
        m1, m2, m3, m4, g1, g2, g3, ua, ub, u2, r1, rb_right, rb_left, [rc_right, rc_left],
    ):
        for copy in copies:
            copy.wait_send()

    def drain(step):
        for stream in (0, 1):
            for way in (RIGHT, LEFT):
                hop(stream, way, step).wait_send()

    loop(0, steps - 1, drain)
    for pair in longer:
        hop(*pair, steps - 1).wait_send()
    for copy in outs:
        copy.wait()
    loop(0, nz, lambda block: finished(block).wait_send())
    loop(0, nz, lambda block: finished(block).wait_recv())
    own.wait()


def per_device(
    n_section, nz, saved_input, norm_gain, down_proj, up_proj, left_in, right_in, warm_right,
    error_buffer, pair_lengths,
):
    tok, feat = saved_input.shape[1:]
    rank = left_in.shape[2]
    rl = down_proj.shape[2]
    half = feat // 2
    steps = nz // 2
    nb = 4
    na = nz // nb
    hbm = pl.BlockSpec(memory_space=pl.ANY)
    dma = pltpu.SemaphoreType.DMA
    vmem = pltpu.VMEM
    scratch = [
        vmem((1, feat), F32),
        vmem((2 * tok, half), BF16),
        vmem((tok, half), BF16),
        vmem((2 * tok, half), BF16),
        vmem((2 * tok, rank), BF16),
        vmem((rl, tok), BF16),
        vmem((half, rl), BF16),
        vmem((nz, 2, tok, rank), BF16),
        vmem((2 * tok, 128), F32),
        vmem((rl, rank), BF16),
        vmem((nb, rl // nb, rank), BF16),
        vmem((rl // nb, rank), BF16),
        vmem((na, rl // nz, rank), BF16),
        vmem((rl // nz, rank), F32),
        vmem((rl // nz, rank), F32),
        vmem((rl // nz, rank), BF16),
        vmem((rl, rank), BF16),
        vmem((2 * tok, half), BF16),
        vmem((2 * tok, rl), BF16),
        vmem((2 * tok, rl), BF16),
        vmem((2 * tok, rl), F32),
        vmem((2 * tok, rl), BF16),
        vmem((2 * tok, half), F32),
        vmem((2 * tok, half), BF16),
        vmem((2 * tok, rank), F32),
        vmem((2 * tok, rank), F32),
        vmem((2 * tok, rank), F32),
        vmem((rank, rank), F32),
        vmem((nb, rank // nb, rank), F32),
        vmem((rank // nb, rank), F32),
        vmem((na, rank // nb, rank), F32),
        vmem((rank, rank), F32),
        vmem((rank, rank), F32),
        vmem((rank, rank), F32),
        vmem((nb, na, rank, tok), F32),
        vmem((2, na // 2, rank, tok), F32),
        vmem((2, na, rank, tok), F32),
        vmem((na, rank, tok), F32),
        vmem((na, rank, tok), BF16),
        vmem((na, rank, tok), BF16),
        vmem((nb, na, rank, tok), BF16),
        vmem((2 * tok, rank), BF16),
        vmem((tok, rank), BF16),
        vmem((2 * tok, half), BF16),
        dma((9,)), dma((7,)), dma((7,)),
        dma((2, 2, steps)), dma((2, 2, steps)),
        dma((4, 4)), dma((4, 4)), dma((4, 4)), dma((4, 4)),
        dma((8,)), dma((8,)), dma((4,)), dma((4,)), dma((6,)), dma((6,)),
        dma((nz,)), dma((nz,)), dma, dma((2,)), dma((2,)),
    ]
    new_error, left_back, right_back = pl.pallas_call(
        functools.partial(kernel, n_section, nz, rank),
        out_shape=(
            jax.ShapeDtypeStruct((tok, feat), BF16),
            jax.ShapeDtypeStruct((tok, rank), BF16),
            jax.ShapeDtypeStruct((tok, rank), BF16),
        ),
        in_specs=[
            pl.BlockSpec(memory_space=pltpu.SMEM), hbm,
            hbm, hbm, hbm, hbm, hbm, hbm, hbm,
        ],
        out_specs=(hbm, hbm, hbm),
        scratch_shapes=scratch,
        compiler_params=pltpu.CompilerParams(
            collective_id=0, has_side_effects=True, vmem_limit_bytes=60 * 1024 * 1024
        ),
    )(
        pair_lengths, norm_gain, saved_input[0], error_buffer[0], down_proj[0], up_proj[0],
        left_in[0], right_in[0], warm_right[0],
    )
    keep = lax.axis_index("section") < n_section - 1
    left_back = jnp.where(keep, left_back, jnp.zeros_like(left_back))
    right_back = jnp.where(keep, right_back, jnp.zeros_like(right_back))
    return (new_error[None], left_back[None], right_back[None])


def solution(mesh):
    n_section = mesh.shape["section"]
    nz = mesh.shape["seq"] // 2
    return jax.shard_map(
        functools.partial(per_device, n_section, nz),
        mesh=mesh,
        in_specs=(
            P("section", "seq", None),
            P("section", None),
            P("section", "seq", None),
            P("section", None, "seq"),
            P("section", "seq", None),
            P("section", "seq", None),
            P("section", "seq", None),
            P("section", "seq", None),
            P("section", None),
        ),
        out_specs=(P("section", "seq", None), P("section", "seq", None), P("section", "seq", None)),
        check_vma=False,
    )
```

```python
import functools

import jax
import jax.numpy as jnp
from jax import lax
from jax.experimental import pallas as pl
from jax.experimental.pallas import tpu as pltpu
from jax.sharding import PartitionSpec as P

MESH = pl.DeviceIdType.MESH
HIGHEST = lax.Precision.HIGHEST
F32 = jnp.float32
BF16 = jnp.bfloat16
RIGHT, LEFT = 0, 1


def nt(a, b, precision=None):
    return lax.dot_general(
        a, b, (((1,), (1,)), ((), ())), preferred_element_type=F32, precision=precision
    )


def nn(a, b, precision=None):
    return jnp.dot(a, b, preferred_element_type=F32, precision=precision)


def split(a):
    hi = a.astype(BF16)
    return hi, (a - hi.astype(F32)).astype(BF16)


def kernel(
    n_section, nz, rank, lens, gain_in, saved, err, down, up, left, right, warm,
    out_ne, out_l, out_r,
    gain, xall, xoth, eall, lall, upv, dall, rw, ivb,
    mpart, mhalf, ml1, m2s, ml2, mxs, mxr, mown, mfull,
    xg, prs, prr, pre_ref, dpre_ref, mom, mom16, pjs, pjr, pj,
    gpart, gl1, g2s, gl2, gfull, work, linv, ut, ula, ulb, u2s, ul2, rt, ph16, rown, neb,
    ld_sem, x_send, x_recv, a_send, a_recv,
    m_send, m_recv, g_send, g_recv, u_send, u_recv, r_send, r_recv, q_send, q_recv,
    ne_send, ne_recv, ne_loc, sec_send, sec_recv,
):
    tok = left.shape[0]
    feat = saved.shape[1]
    half = feat // 2
    steps = nz // 2
    chunk = 2 * tok
    n_chunk = half // chunk
    rl = down.shape[1]
    nb = 4
    na = nz // nb

    s = lax.axis_index("section")
    q = lax.axis_index("seq")
    x = q // nz
    z = lax.rem(q, nz)
    a = z // nb
    b = lax.rem(z, nb)
    o = 1 - x
    base = x * nz
    partner = o * nz + z
    zr = base + lax.rem(z + 1, nz)
    zl = base + lax.rem(z + nz - 1, nz)
    s_prev = lax.rem(s + n_section - 1, n_section)
    s_next = lax.rem(s + 1, n_section)

    def mod(i):
        return lax.rem(i + 2 * nz, nz)

    def rows(start, size):
        return pl.ds(pl.multiple_of(start, size), size)

    def near_b(k):
        return lax.rem(b + k, nb)

    def far_a(k):
        return lax.rem(a + k, na)

    mine = rows(x * tok, tok)
    theirs = rows(o * tok, tok)
    my_half = rows(x * half, half)
    other_half = rows(o * half, half)
    my_block = rows(z * tok, tok)

    loads = [
        pltpu.make_async_copy(src, dst, ld_sem.at[i])
        for i, (src, dst) in enumerate([
            (down, dall.at[my_block]),
            (right, rw.at[z, 0]),
            (warm, rw.at[z, 1]),
            (left, lall.at[mine]),
            (saved.at[:, other_half], xoth),
            (up, upv),
            (saved.at[:, my_half], xall.at[mine]),
            (err.at[:, my_half], eall.at[mine]),
            (gain_in, gain),
        ])
    ]
    for load in loads:
        load.start()

    barrier = pltpu.get_barrier_semaphore()
    peers = [{"seq": base + a * nb + near_b(k)} for k in range(1, nb)]
    peers += [{"seq": base + far_a(k) * nb + b} for k in range(1, na)]
    peers += [{"seq": zr}, {"seq": zl}, {"seq": partner}, {"section": s_prev}, {"section": s_next}]
    for peer in peers:
        pl.semaphore_signal(barrier, inc=1, device_id=peer, device_id_type=MESH)
    pl.semaphore_wait(barrier, len(peers))

    def send_to(device, src, dst, send, recv):
        return pltpu.make_async_remote_copy(
            src_ref=src, dst_ref=dst, send_sem=send, recv_sem=recv,
            device_id=device, device_id_type=MESH,
        )

    def across(i, src, dst):
        return send_to({"seq": partner}, src, dst, x_send.at[i], x_recv.at[i])

    def near(k, src, dst, send, recv):
        return send_to({"seq": base + a * nb + near_b(k)}, src, dst, send, recv)

    def far(k, src, dst, send, recv):
        return send_to({"seq": base + far_a(k) * nb + b}, src, dst, send, recv)

    def loop(first, end, fn):
        def body(k, _):
            fn(k)
            return 0

        lax.fori_loop(first, end, body, 0)

    longer = [(0, RIGHT), (1, LEFT)]

    def hop(stream, way, step):
        block = mod(z - step) if way == RIGHT else mod(z + step)
        ref = dall.at[rows(block * tok, tok)] if stream == 0 else rw.at[block]
        return send_to(
            {"seq": zr if way == RIGHT else zl}, ref, ref,
            a_send.at[stream, way, step], a_recv.at[stream, way, step],
        )

    def has(stream, way, step):
        return step < (steps if (stream, way) in longer else steps - 1)

    def advance(stream, step):
        for way in (RIGHT, LEFT):
            if has(stream, way, step):
                hop(stream, way, step).wait_recv()
                if has(stream, way, step + 1):
                    hop(stream, way, step + 1).start()

    def ring_start(stream):
        for way in (RIGHT, LEFT):
            hop(stream, way, 0).start()

    loads[0].wait()
    ring_start(0)
    loads[1].wait()
    loads[2].wait()
    loads[3].wait()
    x_left = across(1, lall.at[mine], lall.at[mine])
    x_left.start()
    loads[5].wait()

    mh, mb, ms = rl // 2, rl // 2 // nb, rl // 2 // nz
    mpart[...] = nn(upv[...], rw[z, 0])
    mxs[...] = mpart[rows(o * mh, mh), :].astype(BF16)
    x_m = across(4, mxs, mxr)
    x_m.start()
    loads[4].wait()
    x_saved = across(0, xoth, xall.at[mine])
    x_saved.start()
    my_mh = rows(x * mh, mh)
    my_mb = pl.ds(pl.multiple_of(x * mh + b * mb, mb), mb)
    my_m = pl.ds(pl.multiple_of(x * mh + b * mb + a * ms, ms), ms)
    m1 = [near(k, mhalf.at[rows(near_b(k) * mb, mb)], ml1.at[k], m_send.at[0, k], m_recv.at[0, k])
          for k in range(1, nb)]
    m2 = [far(k, m2s.at[rows(far_a(k) * ms, ms)], ml2.at[k], m_send.at[1, k], m_recv.at[1, k])
          for k in range(1, na)]
    m3 = [far(k, mown, mfull.at[my_m], m_send.at[2, k], m_recv.at[2, k]) for k in range(1, na)]
    m4 = [near(k, mfull.at[my_mb], mfull.at[my_mb], m_send.at[3, k], m_recv.at[3, k])
          for k in range(1, nb)]

    def start(copies):
        for copy in copies:
            copy.start()

    def arrive(copies):
        for copy in copies:
            copy.wait_recv()

    x_err = across(2, err.at[:, other_half], eall.at[mine])
    x_err.start()

    loads[6].wait()
    total = jnp.zeros((tok, 1), F32)
    for c in range(half // 512):
        cols = pl.ds(c * 512, 512)
        for v in (xoth[:, cols], xall[mine, cols]):
            v = v.astype(F32)
            total = total + jnp.sum(v * v, axis=1, keepdims=True)
    ivb[mine, :] = jnp.broadcast_to(lax.rsqrt(total * (1.0 / feat) + 1e-05), (tok, 128))
    x_inv = across(3, ivb.at[mine], ivb.at[mine])
    x_inv.start()

    gain_off = x * half

    def scale(c):
        cols = rows(c * chunk, chunk)
        g = gain[:, rows(gain_off + c * chunk, chunk)]
        xg[:, cols] = (xall[:, cols].astype(F32) * g).astype(BF16)

    def term(block):
        return nn(xg[:, rows(block * tok, tok)], dall[rows(block * tok, tok), :])

    def blocks_of(step):
        if step < 0:
            return [z]
        if step == steps - 1:
            return [mod(z - steps)]
        return [mod(z - 1 - step), mod(z + 1 + step)]

    lag = 3 * steps // 8
    for t in range(steps):
        if t == lag:
            ring_start(1)
        advance(0, t)
        if t >= lag:
            advance(1, t - lag)
        if t == steps // 8:
            x_m.wait_recv()
            mhalf[...] = (mpart[my_mh, :] + mxr[...].astype(F32)).astype(BF16)
            start(m1)
        if t == 3 * steps // 8:
            arrive(m1)
            msum = mhalf[rows(b * mb, mb), :].astype(F32)
            for k in range(1, nb):
                msum = msum + ml1[k].astype(F32)
            m2s[...] = msum.astype(BF16)
            start(m2)
        if t == 5 * steps // 8:
            arrive(m2)
            msum = m2s[rows(a * ms, ms), :].astype(F32)
            for k in range(1, na):
                msum = msum + ml2[k].astype(F32)
            mown[...] = msum.astype(BF16)
            mfull[my_m, :] = mown[...]
            start(m3)
        if t == steps // 2:
            x_saved.wait_recv()
            loads[8].wait()
            loop(0, n_chunk, scale)
            pre_ref[...] = term(z)
        if t == 6 * steps // 8:
            arrive(m3)
            start(m4)
        if t == 7 * steps // 8:
            arrive(m4)
            x_m2 = across(7, mfull.at[my_mh], mfull.at[my_mh])
            x_m2.start()
        if t >= steps // 2:
            first = 2 * (t - steps // 2)
            found = [term(block) for step in (first, first + 1) for block in blocks_of(step)]
            pre_own = pre_ref[...] + sum(found[1:], found[0])
            pre_ref[...] = pre_own
    prs[...] = pre_own.astype(BF16)
    x_pre = across(5, prs, prr)
    x_pre.start()

    x_left.wait_recv()
    share = -(-(steps + 1) // lag)
    for i in range(lag):
        advance(1, steps - lag + i)
        for step in range(i * share - 1, min((i + 1) * share, steps + 1) - 1):
            for block in blocks_of(step):
                mom[:, rows(block * tok, tok)] = nt(lall[...], rw[block, 0])
    x_inv.wait_recv()
    x_m2.wait_recv()
    dact = nt(lall[...], mfull[...])
    inv = ivb[:, 0:1]
    slot = z * tok + lax.broadcasted_iota(jnp.int32, (2 * tok, 1), 0)
    second = lax.broadcasted_iota(jnp.int32, (2 * tok, 1), 0) >= tok
    limit = jnp.where(second, lens[0, 1] + tok, lens[0, 0])
    live = jnp.where(slot < limit, 1.0, 0.0).astype(F32)

    loads[7].wait()
    x_err.wait_recv()
    x_pre.wait_recv()
    pre = inv * (pre_ref[...] + prr[...].astype(F32))
    sg = 1.0 / (1.0 + jnp.exp(-pre))
    dpre = (dact * sg * (1.0 + pre * (1.0 - sg))).astype(BF16)
    dpre_ref[...] = dpre
    mean = jnp.sum(dpre.astype(F32) * pre, axis=1, keepdims=True) * (1.0 / feat)
    back = inv * inv * mean
    pjs[...] = jnp.zeros_like(pjs)

    def momentum(c):
        cols = rows(c * chunk, chunk)
        g = gain[:, rows(gain_off + c * chunk, chunk)]
        dn = nt(dpre_ref[...], dall[cols, :])
        m = mom[:, cols] + eall[:, cols].astype(F32)
        m = live * (m + inv * (dn * g) - xall[:, cols].astype(F32) * back)
        mom[:, cols] = m
        m16 = m.astype(BF16)
        mom16[:, cols] = m16
        pjs[...] += nn(m16, rw[pl.ds(2 * c, 2), 1].reshape(chunk, rank))

    loop(0, n_chunk, momentum)
    x_pj = across(6, pjs, pjr)
    x_pj.start()
    x_pj.wait_recv()
    proj = pjs[...] + pjr[...]
    pj[...] = proj
    proj_t = proj.T

    gb = rank // nb
    my_gb = rows(b * gb, gb)
    gpart[...] = nn(proj_t, proj, HIGHEST)
    g1 = [near(k, gpart.at[rows(near_b(k) * gb, gb)], gl1.at[k], g_send.at[0, k], g_recv.at[0, k])
          for k in range(1, nb)]
    g2 = [far(k, g2s, gl2.at[k], g_send.at[1, k], g_recv.at[1, k]) for k in range(1, na)]
    g3 = [near(k, gfull.at[my_gb], gfull.at[my_gb], g_send.at[2, k], g_recv.at[2, k])
          for k in range(1, nb)]
    start(g1)

    hi, lo = split(proj_t)

    def moment_terms(j):
        residue = near_b(j)

        def terms(i):
            m = mom16[:, rows((i * nb + residue) * tok, tok)]
            ut[residue, i] = nn(hi, m) + nn(lo, m)

        loop(0, na, terms)

    first_half, last_half = pl.ds(0, na // 2), pl.ds(na // 2, na // 2)
    to_right, to_left = {"seq": zr}, {"seq": zl}
    ua = [
        send_to(to_right, ut.at[near_b(2), first_half], ula.at[0], u_send.at[0], u_recv.at[0]),
        send_to(to_left, ut.at[near_b(2), last_half], ula.at[1], u_send.at[1], u_recv.at[1]),
    ]
    ub = [
        send_to(to_right, ut.at[near_b(1)], ulb.at[0], u_send.at[2], u_recv.at[2]),
        send_to(to_left, ut.at[near_b(3)], ulb.at[1], u_send.at[3], u_recv.at[3]),
    ]
    u2 = [far(k, u2s.at[far_a(k)], ul2.at[k], u_send.at[3 + k], u_recv.at[3 + k])
          for k in range(1, na)]

    moment_terms(2)
    start(ua)
    arrive(g1)
    gsum = gpart[my_gb, :]
    for k in range(1, nb):
        gsum = gsum + gl1[k]
    g2s[...] = gsum
    start(g2)
    moment_terms(1)
    moment_terms(3)
    arrive(ua)
    ut[near_b(1), first_half] += ula[0]
    ut[near_b(3), last_half] += ula[1]
    start(ub)
    moment_terms(0)
    arrive(g2)
    gsum = g2s[...]
    for k in range(1, na):
        gsum = gsum + gl2[k]
    gfull[my_gb, :] = gsum
    start(g3)
    arrive(ub)
    u2s[...] = ut[b] + ulb[0] + ulb[1]
    start(u2)
    arrive(g3)
    work[...] = gfull[...]

    lane = lax.broadcasted_iota(jnp.int32, (1, rank), 1)
    group, width = 16, 8

    def eliminate(first, width):
        n = rank - first
        a = work[pl.ds(first, n), :]
        index = lax.broadcasted_iota(jnp.int32, (n, rank), 0)
        cols = [
            jnp.broadcast_to(a[:, first + k : first + k + 1], (n, rank)) for k in range(width)
        ]
        panel = a[0:8, :]
        rest = jnp.where((lane >= first) & (lane < first + width), 0.0, a)
        for k in range(width):
            here = lane == first + k
            pivot = cols[k][k : k + 1, :]
            factor = jnp.where(index > k, cols[k] * (1.0 / pivot), 0.0)
            unit = jnp.where(here, 1.0, panel[k : k + 1, :])
            linv[first + k : first + k + 1, :] = (
                jnp.where(lane <= first + k, unit, 0.0) * lax.rsqrt(pivot)
            )
            if k + 1 < width:
                panel = jnp.where(here, 0.0, panel) - factor[0:8, :] * unit
            for later in range(k + 1, width):
                cols[later] = cols[later] - factor * cols[k][later : later + 1, :]
            inside = (lane > first + k) & (lane < first + width)
            rest = rest - factor * jnp.where(inside, 0.0, unit)
        if n > width:
            work[pl.ds(first + width, n - width), :] = rest[width:, :]

    for first in range(0, rank, width):
        eliminate(first, width)

    li = linv[...]
    arrive(u2)
    usum = u2s[a]
    for k in range(1, na):
        usum = usum + ul2[k]
    right_t = nn(li, usum, HIGHEST)
    rt[b, a] = right_t.astype(BF16)
    r1 = [far(k, rt.at[b, a], rt.at[b, a], r_send.at[k], r_recv.at[k]) for k in range(1, na)]
    start(r1)
    ph16[...] = nt(pj[...], li, HIGHEST).astype(BF16)
    to_prev = {"section": s_prev}
    outs = [
        send_to(to_prev, ph16.at[mine], out_l, sec_send.at[0], sec_recv.at[0]),
        send_to(to_prev, rown, out_r, sec_send.at[1], sec_recv.at[1]),
    ]
    outs[0].start()
    def pass_on(device, view, i):
        return send_to(device, rt.at[view], rt.at[view], q_send.at[i], q_recv.at[i])

    rb_right = [pass_on(to_right, (b, first_half), 0), pass_on(to_right, (b, last_half), 1)]
    rb_left = [pass_on(to_left, (b, first_half), 2), pass_on(to_left, (b, last_half), 3)]
    rc_right = pass_on(to_right, (near_b(3), first_half), 4)
    rc_left = pass_on(to_left, (near_b(1), last_half), 5)
    rown[...] = right_t.T.astype(BF16)
    outs[1].start()
    arrive(r1)
    start([rb_right[0], rb_left[1], rb_right[1], rb_left[0]])

    def finished(block):
        cols = rows(block * tok, tok)
        return send_to(
            {"seq": partner}, neb.at[theirs, cols], out_ne.at[:, rows(x * half + block * tok, tok)],
            ne_send.at[block], ne_recv.at[block],
        )

    def finish(j, first, end):
        residue = near_b(j)

        def one(i):
            block = i * nb + residue
            cols = rows(block * tok, tok)
            approx = nn(ph16[...], rt[residue, i])
            neb[:, cols] = (mom[:, cols] - approx).astype(BF16)
            finished(block).start()

        loop(first, end, one)

    finish(0, 0, na)
    rb_right[0].wait_recv()
    rc_right.start()
    rb_left[1].wait_recv()
    rc_left.start()
    rb_right[1].wait_recv()
    finish(3, 0, na)
    rb_left[0].wait_recv()
    finish(1, 0, na)
    rc_right.wait_recv()
    finish(2, 0, na // 2)
    rc_left.wait_recv()
    finish(2, na // 2, na)
    own = pltpu.make_async_copy(neb.at[mine], out_ne.at[:, my_half], ne_loc)
    own.start()

    for copy in (x_saved, x_left, x_err, x_inv, x_m, x_m2, x_pre, x_pj):
        copy.wait_send()
    for copies in (
        m1, m2, m3, m4, g1, g2, g3, ua, ub, u2, r1, rb_right, rb_left, [rc_right, rc_left],
    ):
        for copy in copies:
            copy.wait_send()

    def drain(step):
        for stream in (0, 1):
            for way in (RIGHT, LEFT):
                hop(stream, way, step).wait_send()

    loop(0, steps - 1, drain)
    for pair in longer:
        hop(*pair, steps - 1).wait_send()
    for copy in outs:
        copy.wait()
    loop(0, nz, lambda block: finished(block).wait_send())
    loop(0, nz, lambda block: finished(block).wait_recv())
    own.wait()


def per_device(
    n_section, nz, saved_input, norm_gain, down_proj, up_proj, left_in, right_in, warm_right,
    error_buffer, pair_lengths,
):
    tok, feat = saved_input.shape[1:]
    rank = left_in.shape[2]
    rl = down_proj.shape[2]
    half = feat // 2
    steps = nz // 2
    nb = 4
    na = nz // nb
    hbm = pl.BlockSpec(memory_space=pl.ANY)
    dma = pltpu.SemaphoreType.DMA
    vmem = pltpu.VMEM
    scratch = [
        vmem((1, feat), F32),
        vmem((2 * tok, half), BF16),
        vmem((tok, half), BF16),
        vmem((2 * tok, half), BF16),
        vmem((2 * tok, rank), BF16),
        vmem((rl, tok), BF16),
        vmem((half, rl), BF16),
        vmem((nz, 2, tok, rank), BF16),
        vmem((2 * tok, 128), F32),
        vmem((rl, rank), F32),
        vmem((rl // 2, rank), BF16),
        vmem((nb, rl // 2 // nb, rank), BF16),
        vmem((rl // 2 // nb, rank), BF16),
        vmem((na, rl // 2 // nz, rank), BF16),
        vmem((rl // 2, rank), BF16),
        vmem((rl // 2, rank), BF16),
        vmem((rl // 2 // nz, rank), BF16),
        vmem((rl, rank), BF16),
        vmem((2 * tok, half), BF16),
        vmem((2 * tok, rl), BF16),
        vmem((2 * tok, rl), BF16),
        vmem((2 * tok, rl), F32),
        vmem((2 * tok, rl), BF16),
        vmem((2 * tok, half), F32),
        vmem((2 * tok, half), BF16),
        vmem((2 * tok, rank), F32),
        vmem((2 * tok, rank), F32),
        vmem((2 * tok, rank), F32),
        vmem((rank, rank), F32),
        vmem((nb, rank // nb, rank), F32),
        vmem((rank // nb, rank), F32),
        vmem((na, rank // nb, rank), F32),
        vmem((rank, rank), F32),
        vmem((rank, rank), F32),
        vmem((rank, rank), F32),
        vmem((nb, na, rank, tok), F32),
        vmem((2, na // 2, rank, tok), F32),
        vmem((2, na, rank, tok), F32),
        vmem((na, rank, tok), F32),
        vmem((na, rank, tok), F32),
        vmem((nb, na, rank, tok), BF16),
        vmem((2 * tok, rank), BF16),
        vmem((tok, rank), BF16),
        vmem((2 * tok, half), BF16),
        dma((9,)), dma((8,)), dma((8,)),
        dma((2, 2, steps)), dma((2, 2, steps)),
        dma((4, 4)), dma((4, 4)), dma((4, 4)), dma((4, 4)),
        dma((8,)), dma((8,)), dma((4,)), dma((4,)), dma((6,)), dma((6,)),
        dma((nz,)), dma((nz,)), dma, dma((2,)), dma((2,)),
    ]
    new_error, left_back, right_back = pl.pallas_call(
        functools.partial(kernel, n_section, nz, rank),
        out_shape=(
            jax.ShapeDtypeStruct((tok, feat), BF16),
            jax.ShapeDtypeStruct((tok, rank), BF16),
            jax.ShapeDtypeStruct((tok, rank), BF16),
        ),
        in_specs=[
            pl.BlockSpec(memory_space=pltpu.SMEM), hbm,
            hbm, hbm, hbm, hbm, hbm, hbm, hbm,
        ],
        out_specs=(hbm, hbm, hbm),
        scratch_shapes=scratch,
        compiler_params=pltpu.CompilerParams(
            collective_id=0, has_side_effects=True, vmem_limit_bytes=60 * 1024 * 1024
        ),
    )(
        pair_lengths, norm_gain, saved_input[0], error_buffer[0], down_proj[0], up_proj[0],
        left_in[0], right_in[0], warm_right[0],
    )
    keep = lax.axis_index("section") < n_section - 1
    left_back = jnp.where(keep, left_back, jnp.zeros_like(left_back))
    right_back = jnp.where(keep, right_back, jnp.zeros_like(right_back))
    return (new_error[None], left_back[None], right_back[None])


def solution(mesh):
    n_section = mesh.shape["section"]
    nz = mesh.shape["seq"] // 2
    return jax.shard_map(
        functools.partial(per_device, n_section, nz),
        mesh=mesh,
        in_specs=(
            P("section", "seq", None),
            P("section", None),
            P("section", "seq", None),
            P("section", None, "seq"),
            P("section", "seq", None),
            P("section", "seq", None),
            P("section", "seq", None),
            P("section", "seq", None),
            P("section", None),
        ),
        out_specs=(P("section", "seq", None), P("section", "seq", None), P("section", "seq", None)),
        check_vma=False,
    )
```

```python
import functools

import jax
import jax.numpy as jnp
from jax import lax
from jax.experimental import pallas as pl
from jax.experimental.pallas import tpu as pltpu
from jax.sharding import PartitionSpec as P

MESH = pl.DeviceIdType.MESH
HIGHEST = lax.Precision.HIGHEST
F32 = jnp.float32
BF16 = jnp.bfloat16
RIGHT, LEFT = 0, 1


def nt(a, b, precision=None):
    return lax.dot_general(
        a, b, (((1,), (1,)), ((), ())), preferred_element_type=F32, precision=precision
    )


def nn(a, b, precision=None):
    return jnp.dot(a, b, preferred_element_type=F32, precision=precision)


def split(a):
    hi = a.astype(BF16)
    return hi, (a - hi.astype(F32)).astype(BF16)


def kernel(
    n_section, nz, rank, lens, gain_in, saved, err, down, up, left, right, warm,
    out_ne, out_l, out_r,
    gain, xall, xoth, eall, lall, upv, dall, rw, ivb, ivs, ivr,
    mpart, mhalf, ml1, m2s, ml2, mxs, mxr, mown, mfull,
    xg, prs, prr, pre_ref, dpre_ref, mom, mom16, pjs, pjr, pj,
    gpart, gl1, g2s, gl2, gfull, work, linv, beyond, ut, ula, ulb, u2s, ul2, rt, ph16, rown, neb,
    ld_sem, x_send, x_recv, a_send, a_recv,
    m_send, m_recv, g_send, g_recv, u_send, u_recv, r_send, r_recv, q_send, q_recv,
    ne_send, ne_recv, ne_loc, sec_send, sec_recv,
):
    tok = left.shape[0]
    feat = saved.shape[1]
    half = feat // 2
    steps = nz // 2
    chunk = 2 * tok
    n_chunk = half // chunk
    rl = down.shape[1]
    nb = 4
    na = nz // nb

    s = lax.axis_index("section")
    q = lax.axis_index("seq")
    x = q // nz
    z = lax.rem(q, nz)
    a = z // nb
    b = lax.rem(z, nb)
    o = 1 - x
    base = x * nz
    partner = o * nz + z
    zr = base + lax.rem(z + 1, nz)
    zl = base + lax.rem(z + nz - 1, nz)
    s_prev = lax.rem(s + n_section - 1, n_section)
    s_next = lax.rem(s + 1, n_section)

    def mod(i):
        return lax.rem(i + 2 * nz, nz)

    def rows(start, size):
        return pl.ds(pl.multiple_of(start, size), size)

    def near_b(k):
        return lax.rem(b + k, nb)

    def far_a(k):
        return lax.rem(a + k, na)

    mine = rows(x * tok, tok)
    theirs = rows(o * tok, tok)
    my_half = rows(x * half, half)
    other_half = rows(o * half, half)
    my_block = rows(z * tok, tok)

    loads = [
        pltpu.make_async_copy(src, dst, ld_sem.at[i])
        for i, (src, dst) in enumerate([
            (down, dall.at[my_block]),
            (right, rw.at[z, 0]),
            (warm, rw.at[z, 1]),
            (left, lall.at[mine]),
            (saved.at[:, other_half], xoth),
            (up, upv),
            (saved.at[:, my_half], xall.at[mine]),
            (err.at[:, my_half], eall.at[mine]),
            (gain_in, gain),
        ])
    ]
    for load in loads:
        load.start()

    barrier = pltpu.get_barrier_semaphore()
    peers = [{"seq": base + a * nb + near_b(k)} for k in range(1, nb)]
    peers += [{"seq": base + far_a(k) * nb + b} for k in range(1, na)]
    peers += [{"seq": zr}, {"seq": zl}, {"seq": partner}, {"section": s_prev}, {"section": s_next}]
    for peer in peers:
        pl.semaphore_signal(barrier, inc=1, device_id=peer, device_id_type=MESH)
    pl.semaphore_wait(barrier, len(peers))

    def send_to(device, src, dst, send, recv):
        return pltpu.make_async_remote_copy(
            src_ref=src, dst_ref=dst, send_sem=send, recv_sem=recv,
            device_id=device, device_id_type=MESH,
        )

    def across(i, src, dst):
        return send_to({"seq": partner}, src, dst, x_send.at[i], x_recv.at[i])

    def near(k, src, dst, send, recv):
        return send_to({"seq": base + a * nb + near_b(k)}, src, dst, send, recv)

    def far(k, src, dst, send, recv):
        return send_to({"seq": base + far_a(k) * nb + b}, src, dst, send, recv)

    def loop(first, end, fn):
        def body(k, _):
            fn(k)
            return 0

        lax.fori_loop(first, end, body, 0)

    longer = [(0, RIGHT), (1, LEFT)]

    def hop(stream, way, step):
        block = mod(z - step) if way == RIGHT else mod(z + step)
        ref = dall.at[rows(block * tok, tok)] if stream == 0 else rw.at[block]
        return send_to(
            {"seq": zr if way == RIGHT else zl}, ref, ref,
            a_send.at[stream, way, step], a_recv.at[stream, way, step],
        )

    def has(stream, way, step):
        return step < (steps if (stream, way) in longer else steps - 1)

    def advance(stream, step):
        for way in (RIGHT, LEFT):
            if has(stream, way, step):
                hop(stream, way, step).wait_recv()
                if has(stream, way, step + 1):
                    hop(stream, way, step + 1).start()

    def ring_start(stream):
        for way in (RIGHT, LEFT):
            hop(stream, way, 0).start()

    loads[0].wait()
    ring_start(0)
    loads[1].wait()
    loads[2].wait()
    loads[3].wait()
    x_left = across(1, lall.at[mine], lall.at[mine])
    x_left.start()
    loads[5].wait()

    mh, mb, ms = rl // 2, rl // 2 // nb, rl // 2 // nz
    mpart[...] = nn(upv[...], rw[z, 0])
    mxs[...] = mpart[rows(o * mh, mh), :].astype(BF16)
    x_m = across(4, mxs, mxr)
    x_m.start()
    loads[4].wait()
    x_saved = across(0, xoth, xall.at[mine])
    x_saved.start()
    my_mh = rows(x * mh, mh)
    my_mb = pl.ds(pl.multiple_of(x * mh + b * mb, mb), mb)
    my_m = pl.ds(pl.multiple_of(x * mh + b * mb + a * ms, ms), ms)
    m1 = [near(k, mhalf.at[rows(near_b(k) * mb, mb)], ml1.at[k], m_send.at[0, k], m_recv.at[0, k])
          for k in range(1, nb)]
    m2 = [far(k, m2s.at[rows(far_a(k) * ms, ms)], ml2.at[k], m_send.at[1, k], m_recv.at[1, k])
          for k in range(1, na)]
    m3 = [far(k, mown, mfull.at[my_m], m_send.at[2, k], m_recv.at[2, k]) for k in range(1, na)]
    m4 = [near(k, mfull.at[my_mb], mfull.at[my_mb], m_send.at[3, k], m_recv.at[3, k])
          for k in range(1, nb)]

    def start(copies):
        for copy in copies:
            copy.start()

    def arrive(copies):
        for copy in copies:
            copy.wait_recv()

    x_err = across(2, err.at[:, other_half], eall.at[mine])
    x_err.start()

    loads[6].wait()
    total = jnp.zeros((tok, 1), F32)
    for c in range(half // 512):
        cols = pl.ds(c * 512, 512)
        for v in (xoth[:, cols], xall[mine, cols]):
            v = v.astype(F32)
            total = total + jnp.sum(v * v, axis=1, keepdims=True)
    inv_own = jnp.broadcast_to(lax.rsqrt(total * (1.0 / feat) + 1e-05), (tok, 128))
    ivb[mine, :] = inv_own
    ivs[...] = inv_own.T[0:8, :]
    x_inv = across(3, ivs, ivr)
    x_inv.start()

    gain_off = x * half

    def scale(c):
        cols = rows(c * chunk, chunk)
        g = gain[:, rows(gain_off + c * chunk, chunk)]
        xg[:, cols] = (xall[:, cols].astype(F32) * g).astype(BF16)

    def term(block):
        return nn(xg[:, rows(block * tok, tok)], dall[rows(block * tok, tok), :])

    def blocks_of(step):
        if step < 0:
            return [z]
        if step == steps - 1:
            return [mod(z - steps)]
        return [mod(z - 1 - step), mod(z + 1 + step)]

    lag = 3 * steps // 8
    for t in range(steps):
        if t == lag:
            ring_start(1)
        advance(0, t)
        if t >= lag:
            advance(1, t - lag)
        if t == steps // 8:
            x_m.wait_recv()
            mhalf[...] = (mpart[my_mh, :] + mxr[...].astype(F32)).astype(BF16)
            start(m1)
        if t == 3 * steps // 8:
            arrive(m1)
            msum = mhalf[rows(b * mb, mb), :].astype(F32)
            for k in range(1, nb):
                msum = msum + ml1[k].astype(F32)
            m2s[...] = msum.astype(BF16)
            start(m2)
        if t == 5 * steps // 8:
            arrive(m2)
            msum = m2s[rows(a * ms, ms), :].astype(F32)
            for k in range(1, na):
                msum = msum + ml2[k].astype(F32)
            mown[...] = msum.astype(BF16)
            mfull[my_m, :] = mown[...]
            start(m3)
        if t == steps // 2:
            x_saved.wait_recv()
            loads[8].wait()
            loop(0, n_chunk, scale)
            pre_ref[...] = term(z)
        if t == 6 * steps // 8:
            arrive(m3)
            start(m4)
        if t == 7 * steps // 8:
            arrive(m4)
            x_m2 = across(7, mfull.at[my_mh], mfull.at[my_mh])
            x_m2.start()
        if t >= steps // 2:
            first = 2 * (t - steps // 2)
            found = [term(block) for step in (first, first + 1) for block in blocks_of(step)]
            pre_own = pre_ref[...] + sum(found[1:], found[0])
            pre_ref[...] = pre_own
    prs[...] = pre_own.astype(BF16)
    x_pre = across(5, prs, prr)
    x_pre.start()

    x_left.wait_recv()
    share = -(-(steps + 1) // lag)
    for i in range(lag):
        advance(1, steps - lag + i)
        for step in range(i * share - 1, min((i + 1) * share, steps + 1) - 1):
            for block in blocks_of(step):
                mom[:, rows(block * tok, tok)] = nt(lall[...], rw[block, 0])
    x_inv.wait_recv()
    ivb[theirs, :] = jnp.broadcast_to(ivr[0:1, :], (tok, 128)).T
    x_m2.wait_recv()
    dact = nt(lall[...], mfull[...])
    inv = ivb[:, 0:1]
    slot = z * tok + lax.broadcasted_iota(jnp.int32, (2 * tok, 1), 0)
    second = lax.broadcasted_iota(jnp.int32, (2 * tok, 1), 0) >= tok
    limit = jnp.where(second, lens[0, 1] + tok, lens[0, 0])
    live = jnp.where(slot < limit, 1.0, 0.0).astype(F32)

    loads[7].wait()
    x_err.wait_recv()
    x_pre.wait_recv()
    pre = inv * (pre_ref[...] + prr[...].astype(F32))
    sg = 1.0 / (1.0 + jnp.exp(-pre))
    dpre = (dact * sg * (1.0 + pre * (1.0 - sg))).astype(BF16)
    dpre_ref[...] = dpre
    mean = jnp.sum(dpre.astype(F32) * pre, axis=1, keepdims=True) * (1.0 / feat)
    back = inv * inv * mean
    pjs[...] = jnp.zeros_like(pjs)

    def momentum(c):
        cols = rows(c * chunk, chunk)
        g = gain[:, rows(gain_off + c * chunk, chunk)]
        dn = nt(dpre_ref[...], dall[cols, :])
        m = mom[:, cols] + eall[:, cols].astype(F32)
        m = live * (m + inv * (dn * g) - xall[:, cols].astype(F32) * back)
        mom[:, cols] = m
        m16 = m.astype(BF16)
        mom16[:, cols] = m16
        pjs[...] += nn(m16, rw[pl.ds(2 * c, 2), 1].reshape(chunk, rank))

    loop(0, n_chunk, momentum)
    x_pj = across(6, pjs, pjr)
    x_pj.start()
    x_pj.wait_recv()
    proj = pjs[...] + pjr[...]
    pj[...] = proj
    proj_t = proj.T

    gb = rank // nb
    my_gb = rows(b * gb, gb)
    gpart[...] = nn(proj_t, proj, HIGHEST)
    g1 = [near(k, gpart.at[rows(near_b(k) * gb, gb)], gl1.at[k], g_send.at[0, k], g_recv.at[0, k])
          for k in range(1, nb)]
    g2 = [far(k, g2s, gl2.at[k], g_send.at[1, k], g_recv.at[1, k]) for k in range(1, na)]
    g3 = [near(k, gfull.at[my_gb], gfull.at[my_gb], g_send.at[2, k], g_recv.at[2, k])
          for k in range(1, nb)]
    start(g1)

    hi, lo = split(proj_t)

    def moment_terms(j):
        residue = near_b(j)

        def terms(i):
            m = mom16[:, rows((i * nb + residue) * tok, tok)]
            ut[residue, i] = nn(hi, m) + nn(lo, m)

        loop(0, na, terms)

    first_half, last_half = pl.ds(0, na // 2), pl.ds(na // 2, na // 2)
    to_right, to_left = {"seq": zr}, {"seq": zl}
    ua = [
        send_to(to_right, ut.at[near_b(2), first_half], ula.at[0], u_send.at[0], u_recv.at[0]),
        send_to(to_left, ut.at[near_b(2), last_half], ula.at[1], u_send.at[1], u_recv.at[1]),
    ]
    ub = [
        send_to(to_right, ut.at[near_b(1)], ulb.at[0], u_send.at[2], u_recv.at[2]),
        send_to(to_left, ut.at[near_b(3)], ulb.at[1], u_send.at[3], u_recv.at[3]),
    ]
    u2 = [far(k, u2s.at[far_a(k)], ul2.at[k], u_send.at[3 + k], u_recv.at[3 + k])
          for k in range(1, na)]

    moment_terms(2)
    start(ua)
    arrive(g1)
    gsum = gpart[my_gb, :]
    for k in range(1, nb):
        gsum = gsum + gl1[k]
    g2s[...] = gsum
    start(g2)
    moment_terms(1)
    moment_terms(3)
    arrive(ua)
    ut[near_b(1), first_half] += ula[0]
    ut[near_b(3), last_half] += ula[1]
    start(ub)
    moment_terms(0)
    arrive(g2)
    gsum = g2s[...]
    for k in range(1, na):
        gsum = gsum + gl2[k]
    gfull[my_gb, :] = gsum
    start(g3)
    arrive(ub)
    u2s[...] = ut[b] + ulb[0] + ulb[1]
    start(u2)
    arrive(g3)
    work[...] = gfull[...]

    lane = lax.broadcasted_iota(jnp.int32, (1, rank), 1)
    block, width = 32, 16

    def eliminate(first, width, end):
        n = end - first
        a = work[pl.ds(first, n), :]
        index = lax.broadcasted_iota(jnp.int32, (n, rank), 0)
        cols = [
            jnp.broadcast_to(a[:, first + k : first + k + 1], (n, rank)) for k in range(width)
        ]
        panel = a[0:width, :]
        rest = jnp.where((lane >= first) & (lane < first + width), 0.0, a)
        for k in range(width):
            here = lane == first + k
            pivot = cols[k][k : k + 1, :]
            factor = jnp.where(index > k, cols[k] * (1.0 / pivot), 0.0)
            unit = jnp.where(here, 1.0, panel[k : k + 1, :])
            scaled = unit * lax.rsqrt(pivot)
            linv[first + k : first + k + 1, :] = jnp.where(lane <= first + k, scaled, 0.0)
            beyond[first + k - (end - block) : first + k + 1 - (end - block), :] = (
                jnp.where(lane >= end, scaled, 0.0)
            )
            if k + 1 < width:
                panel = jnp.where(here, 0.0, panel) - factor[0:width, :] * unit
            for later in range(k + 1, width):
                cols[later] = cols[later] - factor * cols[k][later : later + 1, :]
            inside = (lane > first + k) & (lane < first + width)
            rest = rest - factor * jnp.where(inside, 0.0, unit)
        if n > width:
            work[pl.ds(first + width, n - width), :] = rest[width:, :]

    for end in range(block, rank + 1, block):
        for first in range(end - block, end, width):
            eliminate(first, width, end)
        if end < rank:
            over = beyond[...]
            update = nn(over.T, over + linv[end - block : end, :], HIGHEST)
            mine_below = jnp.where((lane >= end - block) & (lane < end), 0.0, work[end:, :])
            work[end:, :] = mine_below - update[end:, :]

    li = linv[...]
    arrive(u2)
    usum = u2s[a]
    for k in range(1, na):
        usum = usum + ul2[k]
    right_t = nn(li, usum, HIGHEST)
    rt[b, a] = right_t.astype(BF16)
    r1 = [far(k, rt.at[b, a], rt.at[b, a], r_send.at[k], r_recv.at[k]) for k in range(1, na)]
    start(r1)
    ph16[...] = nt(pj[...], li, HIGHEST).astype(BF16)
    to_prev = {"section": s_prev}
    outs = [
        send_to(to_prev, ph16.at[mine], out_l, sec_send.at[0], sec_recv.at[0]),
        send_to(to_prev, rown, out_r, sec_send.at[1], sec_recv.at[1]),
    ]
    outs[0].start()
    def pass_on(device, view, i):
        return send_to(device, rt.at[view], rt.at[view], q_send.at[i], q_recv.at[i])

    rb_right = [pass_on(to_right, (b, first_half), 0), pass_on(to_right, (b, last_half), 1)]
    rb_left = [pass_on(to_left, (b, first_half), 2), pass_on(to_left, (b, last_half), 3)]
    rc_right = pass_on(to_right, (near_b(3), first_half), 4)
    rc_left = pass_on(to_left, (near_b(1), last_half), 5)
    rown[...] = right_t.T.astype(BF16)
    outs[1].start()
    arrive(r1)
    start([rb_right[0], rb_left[1], rb_right[1], rb_left[0]])

    def finished(block):
        cols = rows(block * tok, tok)
        return send_to(
            {"seq": partner}, neb.at[theirs, cols], out_ne.at[:, rows(x * half + block * tok, tok)],
            ne_send.at[block], ne_recv.at[block],
        )

    def finish(j, first, end):
        residue = near_b(j)

        def one(i):
            block = i * nb + residue
            cols = rows(block * tok, tok)
            approx = nn(ph16[...], rt[residue, i])
            neb[:, cols] = (mom[:, cols] - approx).astype(BF16)
            finished(block).start()

        loop(first, end, one)

    finish(0, 0, na)
    rb_right[0].wait_recv()
    rc_right.start()
    rb_left[1].wait_recv()
    rc_left.start()
    rb_right[1].wait_recv()
    finish(3, 0, na)
    rb_left[0].wait_recv()
    finish(1, 0, na)
    rc_right.wait_recv()
    finish(2, 0, na // 2)
    rc_left.wait_recv()
    finish(2, na // 2, na)
    own = pltpu.make_async_copy(neb.at[mine], out_ne.at[:, my_half], ne_loc)
    own.start()

    for copy in (x_saved, x_left, x_err, x_inv, x_m, x_m2, x_pre, x_pj):
        copy.wait_send()
    for copies in (
        m1, m2, m3, m4, g1, g2, g3, ua, ub, u2, r1, rb_right, rb_left, [rc_right, rc_left],
    ):
        for copy in copies:
            copy.wait_send()

    def drain(step):
        for stream in (0, 1):
            for way in (RIGHT, LEFT):
                hop(stream, way, step).wait_send()

    loop(0, steps - 1, drain)
    for pair in longer:
        hop(*pair, steps - 1).wait_send()
    for copy in outs:
        copy.wait()
    loop(0, nz, lambda block: finished(block).wait_send())
    loop(0, nz, lambda block: finished(block).wait_recv())
    own.wait()


def per_device(
    n_section, nz, saved_input, norm_gain, down_proj, up_proj, left_in, right_in, warm_right,
    error_buffer, pair_lengths,
):
    tok, feat = saved_input.shape[1:]
    rank = left_in.shape[2]
    rl = down_proj.shape[2]
    half = feat // 2
    steps = nz // 2
    nb = 4
    na = nz // nb
    hbm = pl.BlockSpec(memory_space=pl.ANY)
    dma = pltpu.SemaphoreType.DMA
    vmem = pltpu.VMEM
    scratch = [
        vmem((1, feat), F32),
        vmem((2 * tok, half), BF16),
        vmem((tok, half), BF16),
        vmem((2 * tok, half), BF16),
        vmem((2 * tok, rank), BF16),
        vmem((rl, tok), BF16),
        vmem((half, rl), BF16),
        vmem((nz, 2, tok, rank), BF16),
        vmem((2 * tok, 128), F32),
        vmem((8, tok), F32),
        vmem((8, tok), F32),
        vmem((rl, rank), F32),
        vmem((rl // 2, rank), BF16),
        vmem((nb, rl // 2 // nb, rank), BF16),
        vmem((rl // 2 // nb, rank), BF16),
        vmem((na, rl // 2 // nz, rank), BF16),
        vmem((rl // 2, rank), BF16),
        vmem((rl // 2, rank), BF16),
        vmem((rl // 2 // nz, rank), BF16),
        vmem((rl, rank), BF16),
        vmem((2 * tok, half), BF16),
        vmem((2 * tok, rl), BF16),
        vmem((2 * tok, rl), BF16),
        vmem((2 * tok, rl), F32),
        vmem((2 * tok, rl), BF16),
        vmem((2 * tok, half), F32),
        vmem((2 * tok, half), BF16),
        vmem((2 * tok, rank), F32),
        vmem((2 * tok, rank), F32),
        vmem((2 * tok, rank), F32),
        vmem((rank, rank), F32),
        vmem((nb, rank // nb, rank), F32),
        vmem((rank // nb, rank), F32),
        vmem((na, rank // nb, rank), F32),
        vmem((rank, rank), F32),
        vmem((rank, rank), F32),
        vmem((rank, rank), F32),
        vmem((32, rank), F32),
        vmem((nb, na, rank, tok), F32),
        vmem((2, na // 2, rank, tok), F32),
        vmem((2, na, rank, tok), F32),
        vmem((na, rank, tok), F32),
        vmem((na, rank, tok), F32),
        vmem((nb, na, rank, tok), BF16),
        vmem((2 * tok, rank), BF16),
        vmem((tok, rank), BF16),
        vmem((2 * tok, half), BF16),
        dma((9,)), dma((8,)), dma((8,)),
        dma((2, 2, steps)), dma((2, 2, steps)),
        dma((4, 4)), dma((4, 4)), dma((4, 4)), dma((4, 4)),
        dma((8,)), dma((8,)), dma((4,)), dma((4,)), dma((6,)), dma((6,)),
        dma((nz,)), dma((nz,)), dma, dma((2,)), dma((2,)),
    ]
    new_error, left_back, right_back = pl.pallas_call(
        functools.partial(kernel, n_section, nz, rank),
        out_shape=(
            jax.ShapeDtypeStruct((tok, feat), BF16),
            jax.ShapeDtypeStruct((tok, rank), BF16),
            jax.ShapeDtypeStruct((tok, rank), BF16),
        ),
        in_specs=[
            pl.BlockSpec(memory_space=pltpu.SMEM), hbm,
            hbm, hbm, hbm, hbm, hbm, hbm, hbm,
        ],
        out_specs=(hbm, hbm, hbm),
        scratch_shapes=scratch,
        compiler_params=pltpu.CompilerParams(
            collective_id=0, has_side_effects=True, vmem_limit_bytes=60 * 1024 * 1024
        ),
    )(
        pair_lengths, norm_gain, saved_input[0], error_buffer[0], down_proj[0], up_proj[0],
        left_in[0], right_in[0], warm_right[0],
    )
    keep = lax.axis_index("section") < n_section - 1
    left_back = jnp.where(keep, left_back, jnp.zeros_like(left_back))
    right_back = jnp.where(keep, right_back, jnp.zeros_like(right_back))
    return (new_error[None], left_back[None], right_back[None])


def solution(mesh):
    n_section = mesh.shape["section"]
    nz = mesh.shape["seq"] // 2
    return jax.shard_map(
        functools.partial(per_device, n_section, nz),
        mesh=mesh,
        in_specs=(
            P("section", "seq", None),
            P("section", None),
            P("section", "seq", None),
            P("section", None, "seq"),
            P("section", "seq", None),
            P("section", "seq", None),
            P("section", "seq", None),
            P("section", "seq", None),
            P("section", None),
        ),
        out_specs=(P("section", "seq", None), P("section", "seq", None), P("section", "seq", None)),
        check_vma=False,
    )
```

```python
import functools

import jax
import jax.numpy as jnp
from jax import lax
from jax.experimental import pallas as pl
from jax.experimental.pallas import tpu as pltpu
from jax.sharding import PartitionSpec as P

MESH = pl.DeviceIdType.MESH
HIGHEST = lax.Precision.HIGHEST
F32 = jnp.float32
BF16 = jnp.bfloat16
RIGHT, LEFT = 0, 1


def nt(a, b, precision=None):
    return lax.dot_general(
        a, b, (((1,), (1,)), ((), ())), preferred_element_type=F32, precision=precision
    )


def nn(a, b, precision=None):
    return jnp.dot(a, b, preferred_element_type=F32, precision=precision)


def split(a):
    hi = a.astype(BF16)
    return hi, (a - hi.astype(F32)).astype(BF16)


def kernel(
    n_section, nz, rank, lens, gain_in, saved, err, down, up, left, right, warm,
    out_ne, out_l, out_r,
    gain, xall, xoth, eall, lall, upv, dall, rw, ivb, ivs, ivr,
    mpart, mhalf, ml1, m2s, ml2, mxs, mxr, mown, mfull,
    xg, prs, prr, pre_ref, dpre_ref, mom, mom16, pjs, pjr, pj,
    gpart, gl1, g2s, gl2, gfull, work, linv, beyond, ut, ula, ulb, u2s, ulc, ul2, rt, ph16, rown, neb,
    ld_sem, x_send, x_recv, a_send, a_recv,
    m_send, m_recv, g_send, g_recv, u_send, u_recv, r_send, r_recv, q_send, q_recv,
    ne_send, ne_recv, ne_loc, sec_send, sec_recv,
):
    tok = left.shape[0]
    feat = saved.shape[1]
    half = feat // 2
    steps = nz // 2
    chunk = 2 * tok
    n_chunk = half // chunk
    rl = down.shape[1]
    nb = 4
    na = nz // nb

    s = lax.axis_index("section")
    q = lax.axis_index("seq")
    x = q // nz
    z = lax.rem(q, nz)
    a = z // nb
    b = lax.rem(z, nb)
    o = 1 - x
    base = x * nz
    partner = o * nz + z
    zr = base + lax.rem(z + 1, nz)
    zl = base + lax.rem(z + nz - 1, nz)
    s_prev = lax.rem(s + n_section - 1, n_section)
    s_next = lax.rem(s + 1, n_section)

    def mod(i):
        return lax.rem(i + 2 * nz, nz)

    def rows(start, size):
        return pl.ds(pl.multiple_of(start, size), size)

    def near_b(k):
        return lax.rem(b + k, nb)

    def far_a(k):
        return lax.rem(a + k, na)

    mine = rows(x * tok, tok)
    theirs = rows(o * tok, tok)
    my_half = rows(x * half, half)
    other_half = rows(o * half, half)
    my_block = rows(z * tok, tok)

    loads = [
        pltpu.make_async_copy(src, dst, ld_sem.at[i])
        for i, (src, dst) in enumerate([
            (down, dall.at[my_block]),
            (right, rw.at[z, 0]),
            (warm, rw.at[z, 1]),
            (left, lall.at[mine]),
            (saved.at[:, other_half], xoth),
            (up, upv),
            (saved.at[:, my_half], xall.at[mine]),
            (err.at[:, my_half], eall.at[mine]),
            (gain_in, gain),
        ])
    ]
    for load in loads:
        load.start()

    barrier = pltpu.get_barrier_semaphore()
    peers = [{"seq": base + a * nb + near_b(k)} for k in range(1, nb)]
    peers += [{"seq": base + far_a(k) * nb + b} for k in range(1, na)]
    peers += [{"seq": zr}, {"seq": zl}, {"seq": partner}, {"section": s_prev}, {"section": s_next}]
    for peer in peers:
        pl.semaphore_signal(barrier, inc=1, device_id=peer, device_id_type=MESH)
    pl.semaphore_wait(barrier, len(peers))

    def send_to(device, src, dst, send, recv):
        return pltpu.make_async_remote_copy(
            src_ref=src, dst_ref=dst, send_sem=send, recv_sem=recv,
            device_id=device, device_id_type=MESH,
        )

    def across(i, src, dst):
        return send_to({"seq": partner}, src, dst, x_send.at[i], x_recv.at[i])

    def near(k, src, dst, send, recv):
        return send_to({"seq": base + a * nb + near_b(k)}, src, dst, send, recv)

    def far(k, src, dst, send, recv):
        return send_to({"seq": base + far_a(k) * nb + b}, src, dst, send, recv)

    def loop(first, end, fn):
        def body(k, _):
            fn(k)
            return 0

        lax.fori_loop(first, end, body, 0)

    longer = [(0, RIGHT), (1, LEFT)]

    def hop(stream, way, step):
        block = mod(z - step) if way == RIGHT else mod(z + step)
        ref = dall.at[rows(block * tok, tok)] if stream == 0 else rw.at[block]
        return send_to(
            {"seq": zr if way == RIGHT else zl}, ref, ref,
            a_send.at[stream, way, step], a_recv.at[stream, way, step],
        )

    def has(stream, way, step):
        return step < (steps if (stream, way) in longer else steps - 1)

    def advance(stream, step):
        for way in (RIGHT, LEFT):
            if has(stream, way, step):
                hop(stream, way, step).wait_recv()
                if has(stream, way, step + 1):
                    hop(stream, way, step + 1).start()

    def ring_start(stream):
        for way in (RIGHT, LEFT):
            hop(stream, way, 0).start()

    loads[0].wait()
    ring_start(0)
    loads[1].wait()
    loads[2].wait()
    loads[3].wait()
    x_left = across(1, lall.at[mine], lall.at[mine])
    x_left.start()
    loads[5].wait()

    mh, mb, ms = rl // 2, rl // 2 // nb, rl // 2 // nz
    mpart[...] = nn(upv[...], rw[z, 0])
    mxs[...] = mpart[rows(o * mh, mh), :].astype(BF16)
    x_m = across(4, mxs, mxr)
    x_m.start()
    loads[4].wait()
    x_saved = across(0, xoth, xall.at[mine])
    x_saved.start()
    my_mh = rows(x * mh, mh)
    my_mb = pl.ds(pl.multiple_of(x * mh + b * mb, mb), mb)
    my_m = pl.ds(pl.multiple_of(x * mh + b * mb + a * ms, ms), ms)
    m1 = [near(k, mhalf.at[rows(near_b(k) * mb, mb)], ml1.at[k], m_send.at[0, k], m_recv.at[0, k])
          for k in range(1, nb)]
    m2 = [far(k, m2s.at[rows(far_a(k) * ms, ms)], ml2.at[k], m_send.at[1, k], m_recv.at[1, k])
          for k in range(1, na)]
    m3 = [far(k, mown, mfull.at[my_m], m_send.at[2, k], m_recv.at[2, k]) for k in range(1, na)]
    m4 = [near(k, mfull.at[my_mb], mfull.at[my_mb], m_send.at[3, k], m_recv.at[3, k])
          for k in range(1, nb)]

    def start(copies):
        for copy in copies:
            copy.start()

    def arrive(copies):
        for copy in copies:
            copy.wait_recv()

    x_err = across(2, err.at[:, other_half], eall.at[mine])
    x_err.start()

    loads[6].wait()
    total = jnp.zeros((tok, 1), F32)
    for c in range(half // 512):
        cols = pl.ds(c * 512, 512)
        for v in (xoth[:, cols], xall[mine, cols]):
            v = v.astype(F32)
            total = total + jnp.sum(v * v, axis=1, keepdims=True)
    inv_own = jnp.broadcast_to(lax.rsqrt(total * (1.0 / feat) + 1e-05), (tok, 128))
    ivb[mine, :] = inv_own
    ivs[...] = inv_own.T[0:8, :]
    x_inv = across(3, ivs, ivr)
    x_inv.start()

    gain_off = x * half

    def scale(c):
        cols = rows(c * chunk, chunk)
        g = gain[:, rows(gain_off + c * chunk, chunk)]
        xg[:, cols] = (xall[:, cols].astype(F32) * g).astype(BF16)

    def term(block):
        return nn(xg[:, rows(block * tok, tok)], dall[rows(block * tok, tok), :])

    def blocks_of(step):
        if step < 0:
            return [z]
        if step == steps - 1:
            return [mod(z - steps)]
        return [mod(z - 1 - step), mod(z + 1 + step)]

    lag = 3 * steps // 8
    for t in range(steps):
        if t == lag:
            ring_start(1)
        advance(0, t)
        if t >= lag:
            advance(1, t - lag)
        if t == steps // 8:
            x_m.wait_recv()
            mhalf[...] = (mpart[my_mh, :] + mxr[...].astype(F32)).astype(BF16)
            start(m1)
        if t == 3 * steps // 8:
            arrive(m1)
            msum = mhalf[rows(b * mb, mb), :].astype(F32)
            for k in range(1, nb):
                msum = msum + ml1[k].astype(F32)
            m2s[...] = msum.astype(BF16)
            start(m2)
        if t == 5 * steps // 8:
            arrive(m2)
            msum = m2s[rows(a * ms, ms), :].astype(F32)
            for k in range(1, na):
                msum = msum + ml2[k].astype(F32)
            mown[...] = msum.astype(BF16)
            mfull[my_m, :] = mown[...]
            start(m3)
        if t == steps // 2:
            x_saved.wait_recv()
            loads[8].wait()
            loop(0, n_chunk, scale)
            pre_ref[...] = term(z)
        if t == 6 * steps // 8:
            arrive(m3)
            start(m4)
        if t == 7 * steps // 8:
            arrive(m4)
            x_m2 = across(7, mfull.at[my_mh], mfull.at[my_mh])
            x_m2.start()
        if t >= steps // 2:
            first = 2 * (t - steps // 2)
            found = [term(block) for step in (first, first + 1) for block in blocks_of(step)]
            pre_own = pre_ref[...] + sum(found[1:], found[0])
            pre_ref[...] = pre_own
    prs[...] = pre_own.astype(BF16)
    x_pre = across(5, prs, prr)
    x_pre.start()

    x_left.wait_recv()
    share = -(-(steps + 1) // lag)
    for i in range(lag):
        advance(1, steps - lag + i)
        for step in range(i * share - 1, min((i + 1) * share, steps + 1) - 1):
            for block in blocks_of(step):
                mom[:, rows(block * tok, tok)] = nt(lall[...], rw[block, 0])
    x_inv.wait_recv()
    ivb[theirs, :] = jnp.broadcast_to(ivr[0:1, :], (tok, 128)).T
    x_m2.wait_recv()
    dact = nt(lall[...], mfull[...])
    inv = ivb[:, 0:1]
    slot = z * tok + lax.broadcasted_iota(jnp.int32, (2 * tok, 1), 0)
    second = lax.broadcasted_iota(jnp.int32, (2 * tok, 1), 0) >= tok
    limit = jnp.where(second, lens[0, 1] + tok, lens[0, 0])
    live = jnp.where(slot < limit, 1.0, 0.0).astype(F32)

    loads[7].wait()
    x_err.wait_recv()
    x_pre.wait_recv()
    pre = inv * (pre_ref[...] + prr[...].astype(F32))
    sg = 1.0 / (1.0 + jnp.exp(-pre))
    dpre = (dact * sg * (1.0 + pre * (1.0 - sg))).astype(BF16)
    dpre_ref[...] = dpre
    mean = jnp.sum(dpre.astype(F32) * pre, axis=1, keepdims=True) * (1.0 / feat)
    back = inv * inv * mean
    pjs[...] = jnp.zeros_like(pjs)

    def momentum(c):
        cols = rows(c * chunk, chunk)
        g = gain[:, rows(gain_off + c * chunk, chunk)]
        dn = nt(dpre_ref[...], dall[cols, :])
        m = mom[:, cols] + eall[:, cols].astype(F32)
        m = live * (m + inv * (dn * g) - xall[:, cols].astype(F32) * back)
        mom[:, cols] = m
        m16 = m.astype(BF16)
        mom16[:, cols] = m16
        pjs[...] += nn(m16, rw[pl.ds(2 * c, 2), 1].reshape(chunk, rank))

    loop(0, n_chunk, momentum)
    x_pj = across(6, pjs, pjr)
    x_pj.start()
    x_pj.wait_recv()
    proj = pjs[...] + pjr[...]
    pj[...] = proj
    proj_t = proj.T

    gb = rank // nb
    my_gb = rows(b * gb, gb)
    gpart[...] = nn(proj_t, proj, HIGHEST)
    g1 = [near(k, gpart.at[rows(near_b(k) * gb, gb)], gl1.at[k], g_send.at[0, k], g_recv.at[0, k])
          for k in range(1, nb)]
    g2 = [far(k, g2s, gl2.at[k], g_send.at[1, k], g_recv.at[1, k]) for k in range(1, na)]
    g3 = [near(k, gfull.at[my_gb], gfull.at[my_gb], g_send.at[2, k], g_recv.at[2, k])
          for k in range(1, nb)]
    start(g1)

    hi, lo = split(proj_t)

    def moment_terms(j):
        residue = near_b(j)

        def terms(i):
            m = mom16[:, rows((i * nb + residue) * tok, tok)]
            ut[residue, i] = nn(hi, m) + nn(lo, m)

        loop(0, na, terms)

    first_half, last_half = pl.ds(0, na // 2), pl.ds(na // 2, na // 2)
    to_right, to_left = {"seq": zr}, {"seq": zl}
    ua = [
        send_to(to_right, ut.at[near_b(2), first_half], ula.at[0], u_send.at[0], u_recv.at[0]),
        send_to(to_left, ut.at[near_b(2), last_half], ula.at[1], u_send.at[1], u_recv.at[1]),
    ]
    ub = [
        send_to(to_right, ut.at[near_b(1)], ulb.at[0], u_send.at[2], u_recv.at[2]),
        send_to(to_left, ut.at[near_b(3)], ulb.at[1], u_send.at[3], u_recv.at[3]),
    ]
    between = na == 4
    top, bottom = pl.ds(0, rank // 2), pl.ds(rank // 2, rank // 2)
    uc = [
        far(k, u2s.at[far_a(2), part], ulc.at[i], u_send.at[6 + i], u_recv.at[6 + i])
        for i, (k, part) in enumerate([(1, top), (3, bottom)])
    ] if between else []
    last_k = (1, 3) if between else tuple(range(1, na))
    u2 = [far(k, u2s.at[far_a(k)], ul2.at[k], u_send.at[3 + k - k // 3], u_recv.at[3 + k - k // 3])
          for k in last_k]

    moment_terms(2)
    start(ua)
    arrive(g1)
    gsum = gpart[my_gb, :]
    for k in range(1, nb):
        gsum = gsum + gl1[k]
    g2s[...] = gsum
    start(g2)
    moment_terms(1)
    moment_terms(3)
    arrive(ua)
    ut[near_b(1), first_half] += ula[0]
    ut[near_b(3), last_half] += ula[1]
    start(ub)
    moment_terms(0)
    arrive(g2)
    gsum = g2s[...]
    for k in range(1, na):
        gsum = gsum + gl2[k]
    gfull[my_gb, :] = gsum
    start(g3)
    arrive(ub)
    u2s[...] = ut[b] + ulb[0] + ulb[1]
    start(uc if between else u2)
    arrive(g3)
    work[...] = gfull[...]

    lane = lax.broadcasted_iota(jnp.int32, (1, rank), 1)
    block, width = 32, 16

    def eliminate(first, width, end):
        n = end - first
        a = work[pl.ds(first, n), :]
        index = lax.broadcasted_iota(jnp.int32, (n, rank), 0)
        cols = [
            jnp.broadcast_to(a[:, first + k : first + k + 1], (n, rank)) for k in range(width)
        ]
        panel = a[0:width, :]
        rest = jnp.where((lane >= first) & (lane < first + width), 0.0, a)
        for k in range(width):
            here = lane == first + k
            pivot = cols[k][k : k + 1, :]
            factor = jnp.where(index > k, cols[k] * (1.0 / pivot), 0.0)
            unit = jnp.where(here, 1.0, panel[k : k + 1, :])
            scaled = unit * lax.rsqrt(pivot)
            linv[first + k : first + k + 1, :] = jnp.where(lane <= first + k, scaled, 0.0)
            beyond[first + k - (end - block) : first + k + 1 - (end - block), :] = (
                jnp.where(lane >= end, scaled, 0.0)
            )
            if k + 1 < width:
                panel = jnp.where(here, 0.0, panel) - factor[0:width, :] * unit
            for later in range(k + 1, width):
                cols[later] = cols[later] - factor * cols[k][later : later + 1, :]
            inside = (lane > first + k) & (lane < first + width)
            rest = rest - factor * jnp.where(inside, 0.0, unit)
        if n > width:
            work[pl.ds(first + width, n - width), :] = rest[width:, :]

    for end in range(block, rank + 1, block):
        for first in range(end - block, end, width):
            eliminate(first, width, end)
        if end < rank:
            over = beyond[...]
            update = nn(over.T, over + linv[end - block : end, :], HIGHEST)
            mine_below = jnp.where((lane >= end - block) & (lane < end), 0.0, work[end:, :])
            work[end:, :] = mine_below - update[end:, :]
        if between and end == rank // 2:
            arrive(uc)
            u2s[far_a(1), top] += ulc[0]
            u2s[far_a(3), bottom] += ulc[1]
            start(u2)

    li = linv[...]
    arrive(u2)
    usum = u2s[a]
    for k in last_k:
        usum = usum + ul2[k]
    right_t = nn(li, usum, HIGHEST)
    rt[b, a] = right_t.astype(BF16)
    r1 = [far(k, rt.at[b, a], rt.at[b, a], r_send.at[k], r_recv.at[k]) for k in range(1, na)]
    start(r1)
    ph16[...] = nt(pj[...], li, HIGHEST).astype(BF16)
    to_prev = {"section": s_prev}
    outs = [
        send_to(to_prev, ph16.at[mine], out_l, sec_send.at[0], sec_recv.at[0]),
        send_to(to_prev, rown, out_r, sec_send.at[1], sec_recv.at[1]),
    ]
    outs[0].start()
    def pass_on(device, view, i):
        return send_to(device, rt.at[view], rt.at[view], q_send.at[i], q_recv.at[i])

    rb_right = [pass_on(to_right, (b, first_half), 0), pass_on(to_right, (b, last_half), 1)]
    rb_left = [pass_on(to_left, (b, first_half), 2), pass_on(to_left, (b, last_half), 3)]
    rc_right = pass_on(to_right, (near_b(3), first_half), 4)
    rc_left = pass_on(to_left, (near_b(1), last_half), 5)
    rown[...] = right_t.T.astype(BF16)
    outs[1].start()
    arrive(r1)
    start([rb_right[0], rb_left[1], rb_right[1], rb_left[0]])

    def finished(block):
        cols = rows(block * tok, tok)
        return send_to(
            {"seq": partner}, neb.at[theirs, cols], out_ne.at[:, rows(x * half + block * tok, tok)],
            ne_send.at[block], ne_recv.at[block],
        )

    def finish(j, first, end):
        residue = near_b(j)

        def one(i):
            block = i * nb + residue
            cols = rows(block * tok, tok)
            approx = nn(ph16[...], rt[residue, i])
            neb[:, cols] = (mom[:, cols] - approx).astype(BF16)
            finished(block).start()

        loop(first, end, one)

    finish(0, 0, na)
    rb_right[0].wait_recv()
    rc_right.start()
    rb_left[1].wait_recv()
    rc_left.start()
    rb_right[1].wait_recv()
    finish(3, 0, na)
    rb_left[0].wait_recv()
    finish(1, 0, na)
    rc_right.wait_recv()
    finish(2, 0, na // 2)
    rc_left.wait_recv()
    finish(2, na // 2, na)
    own = pltpu.make_async_copy(neb.at[mine], out_ne.at[:, my_half], ne_loc)
    own.start()

    for copy in (x_saved, x_left, x_err, x_inv, x_m, x_m2, x_pre, x_pj):
        copy.wait_send()
    for copies in (
        m1, m2, m3, m4, g1, g2, g3, ua, ub, uc, u2, r1, rb_right, rb_left, [rc_right, rc_left],
    ):
        for copy in copies:
            copy.wait_send()

    def drain(step):
        for stream in (0, 1):
            for way in (RIGHT, LEFT):
                hop(stream, way, step).wait_send()

    loop(0, steps - 1, drain)
    for pair in longer:
        hop(*pair, steps - 1).wait_send()
    for copy in outs:
        copy.wait()
    loop(0, nz, lambda block: finished(block).wait_send())
    loop(0, nz, lambda block: finished(block).wait_recv())
    own.wait()


def per_device(
    n_section, nz, saved_input, norm_gain, down_proj, up_proj, left_in, right_in, warm_right,
    error_buffer, pair_lengths,
):
    tok, feat = saved_input.shape[1:]
    rank = left_in.shape[2]
    rl = down_proj.shape[2]
    half = feat // 2
    steps = nz // 2
    nb = 4
    na = nz // nb
    hbm = pl.BlockSpec(memory_space=pl.ANY)
    dma = pltpu.SemaphoreType.DMA
    vmem = pltpu.VMEM
    scratch = [
        vmem((1, feat), F32),
        vmem((2 * tok, half), BF16),
        vmem((tok, half), BF16),
        vmem((2 * tok, half), BF16),
        vmem((2 * tok, rank), BF16),
        vmem((rl, tok), BF16),
        vmem((half, rl), BF16),
        vmem((nz, 2, tok, rank), BF16),
        vmem((2 * tok, 128), F32),
        vmem((8, tok), F32),
        vmem((8, tok), F32),
        vmem((rl, rank), F32),
        vmem((rl // 2, rank), BF16),
        vmem((nb, rl // 2 // nb, rank), BF16),
        vmem((rl // 2 // nb, rank), BF16),
        vmem((na, rl // 2 // nz, rank), BF16),
        vmem((rl // 2, rank), BF16),
        vmem((rl // 2, rank), BF16),
        vmem((rl // 2 // nz, rank), BF16),
        vmem((rl, rank), BF16),
        vmem((2 * tok, half), BF16),
        vmem((2 * tok, rl), BF16),
        vmem((2 * tok, rl), BF16),
        vmem((2 * tok, rl), F32),
        vmem((2 * tok, rl), BF16),
        vmem((2 * tok, half), F32),
        vmem((2 * tok, half), BF16),
        vmem((2 * tok, rank), F32),
        vmem((2 * tok, rank), F32),
        vmem((2 * tok, rank), F32),
        vmem((rank, rank), F32),
        vmem((nb, rank // nb, rank), F32),
        vmem((rank // nb, rank), F32),
        vmem((na, rank // nb, rank), F32),
        vmem((rank, rank), F32),
        vmem((rank, rank), F32),
        vmem((rank, rank), F32),
        vmem((32, rank), F32),
        vmem((nb, na, rank, tok), F32),
        vmem((2, na // 2, rank, tok), F32),
        vmem((2, na, rank, tok), F32),
        vmem((na, rank, tok), F32),
        vmem((2, rank // 2, tok), F32),
        vmem((na, rank, tok), F32),
        vmem((nb, na, rank, tok), BF16),
        vmem((2 * tok, rank), BF16),
        vmem((tok, rank), BF16),
        vmem((2 * tok, half), BF16),
        dma((9,)), dma((8,)), dma((8,)),
        dma((2, 2, steps)), dma((2, 2, steps)),
        dma((4, 4)), dma((4, 4)), dma((4, 4)), dma((4, 4)),
        dma((8,)), dma((8,)), dma((4,)), dma((4,)), dma((6,)), dma((6,)),
        dma((nz,)), dma((nz,)), dma, dma((2,)), dma((2,)),
    ]
    new_error, left_back, right_back = pl.pallas_call(
        functools.partial(kernel, n_section, nz, rank),
        out_shape=(
            jax.ShapeDtypeStruct((tok, feat), BF16),
            jax.ShapeDtypeStruct((tok, rank), BF16),
            jax.ShapeDtypeStruct((tok, rank), BF16),
        ),
        in_specs=[
            pl.BlockSpec(memory_space=pltpu.SMEM), hbm,
            hbm, hbm, hbm, hbm, hbm, hbm, hbm,
        ],
        out_specs=(hbm, hbm, hbm),
        scratch_shapes=scratch,
        compiler_params=pltpu.CompilerParams(
            collective_id=0, has_side_effects=True, vmem_limit_bytes=60 * 1024 * 1024
        ),
    )(
        pair_lengths, norm_gain, saved_input[0], error_buffer[0], down_proj[0], up_proj[0],
        left_in[0], right_in[0], warm_right[0],
    )
    keep = lax.axis_index("section") < n_section - 1
    left_back = jnp.where(keep, left_back, jnp.zeros_like(left_back))
    right_back = jnp.where(keep, right_back, jnp.zeros_like(right_back))
    return (new_error[None], left_back[None], right_back[None])


def solution(mesh):
    n_section = mesh.shape["section"]
    nz = mesh.shape["seq"] // 2
    return jax.shard_map(
        functools.partial(per_device, n_section, nz),
        mesh=mesh,
        in_specs=(
            P("section", "seq", None),
            P("section", None),
            P("section", "seq", None),
            P("section", None, "seq"),
            P("section", "seq", None),
            P("section", "seq", None),
            P("section", "seq", None),
            P("section", "seq", None),
            P("section", None),
        ),
        out_specs=(P("section", "seq", None), P("section", "seq", None), P("section", "seq", None)),
        check_vma=False,
    )
```
